128 devices in a mesh: seq: 16 (over z, x_hi, core), exp: 8 (over x_lo, y).
Axes of the slice: x: 4 (x_hi: 2, x_lo: 2; x = x_hi * 2 + x_lo), y: 4, z: 4, core: 2. Of those that a mesh axis runs over, the one named last changes fastest.
Arguments:
- residual: bfloat16 [2048, 6144], P(('seq', 'exp')), may hold values from -3 to 3
- queries: bfloat16 [2048, 6144], P('seq', 'exp'), may hold values from -6 to 6
- key_heads: bfloat16 [2048, 1024], P('seq', 'exp'), may hold values from -6 to 6
- value_heads: bfloat16 [2048, 1024], P('seq', 'exp'), may hold values from -6 to 6
- out_proj: bfloat16 [6144, 6144], P('exp', 'seq'), may hold values from -0.3125 to 0.3125
- norm_gain: float32 [6144], replicated, may hold values from 0.5 to 1.5
- gate_weight: bfloat16 [8, 8192, 6144], P('exp', 'seq'), may hold values from -0.078125 to 0.078125
- up_weight: bfloat16 [8, 8192, 6144], P('exp', 'seq'), may hold values from -0.078125 to 0.078125
- down_weight: bfloat16 [8, 8192, 6144], P('exp', 'seq'), may hold values from -0.0625 to 0.0625
- adapter_in: bfloat16 [8, 1024, 6144], P('exp', 'seq'), may hold values from -0.078125 to 0.078125
- adapter_out: bfloat16 [8, 1024, 6144], P('exp', 'seq'), may hold values from -0.1875 to 0.1875
- route_ids: int32 [2048, 2], P(('seq', 'exp')), may hold values from 0 to 7, all different within a row; in each aligned block of 16 rows (0 to 15, 16 to 31, ...) at most 5 rows name the same one
- route_gates: float32 [2048, 2], P(('seq', 'exp')), may hold values from 0.2 to 1
- adapter_mix: int32 [2048, 64], P(('seq', 'exp')), may hold values from -8 to 8
Outputs:
- mixed: bfloat16 [2048, 6144], P(('seq', 'exp'))
The draws below stay inside these ranges and needn't reach their ends.
Inputs may be any that keep to these rules, and one draw needn't show every extreme that they name: `route_ids`: in each aligned block of 16 rows (the rows of one device) no expert is named more than 5 times, a bound that some block reaches; the two experts of a row differ.
All inputs are finite; a program needn't handle non-finite values.
Results may differ from the reference program's by a relative error of at most 0.023.
Values may be sent and summed in bfloat16 or wider, within the bound.
A program may use at most 128 MiB of HBM per device.

```python
import math
import jax
import jax.numpy as jnp
import numpy as np
from jax import lax

D = 6144
HD = 128
GROUP = 6
FF = 8192
ADAPTERS = 64
RANK = 16
TOK_DEV = 16
EXPERTS = 8
KV_HEADS = 8
HEADS = 48
CAP = 5
LENGTH = 2048


def draw_queries(key, part):
    key = jax.random.fold_in(key, 11)
    return jnp.clip(jax.random.normal(key, (LENGTH, HEADS * HD), jnp.float32), -5.0, 5.0).astype(jnp.bfloat16)


def draw_key_heads(key, part):
    key = jax.random.fold_in(key, 12)
    return jnp.clip(jax.random.normal(key, (LENGTH, KV_HEADS * HD), jnp.float32), -5.0, 5.0).astype(jnp.bfloat16)


def set_ends(values, rng, least, top_value):
    dims = values.shape
    index_at = [jax.random.randint(jax.random.fold_in(rng, axis), (), 0, dims[axis]) for axis in range(len(dims))]
    values = values.at[tuple(index_at)].set(least)
    longest = dims.index(max(dims))
    index_at[longest] = (index_at[longest] + 1) % dims[longest]
    return values.at[tuple(index_at)].set(top_value)


def block_levels(stream_key, dims, pieces, smallest, top_value):
    def one(axis_at, parts):
        draws = jax.random.uniform(jax.random.fold_in(jax.random.fold_in(stream_key, 6), axis_at), (parts,), jnp.float32, smallest / len(pieces), top_value / len(pieces))
        return jnp.repeat(jnp.exp(draws), dims[axis_at] // parts).reshape((-1,) + (1,) * (len(dims) - axis_at - 1))

    loudness = one(*pieces[0])
    for cut in pieces[1:]:
        loudness = loudness * one(*cut)
    return loudness


def deal_out(key, own, number, rows, number_of, top, bound, skew):
    order = jax.random.permutation(key, number_of)
    heavy_load, usual = portions_of(number_of, rows * top, bound, skew, True), portions_of(number_of, rows * top, bound, skew, False)
    places = jnp.arange(number_of)

    def named(sizes, turn):
        used = int((sizes > 0).sum())
        fixed = max(1, used // 4)
        passed = fixed + (places - fixed + turn * (used - fixed)) % max(1, number_of - fixed)
        return jnp.zeros((number_of,), jnp.int32).at[order[jnp.where(places < fixed, places, passed)]].set(jnp.asarray(sizes, jnp.int32))

    sizes = jnp.where(number % 4 == 0, named(heavy_load, number // 4), named(usual, number - number // 4 - 1))
    mixed = jax.random.permutation(jax.random.fold_in(own, 3), number_of)
    source_of, receiver = mixed[0:number_of // 2 * 2:2], mixed[1:number_of // 2 * 2:2]
    margin = jnp.minimum(sizes[source_of] - 1, bound - sizes[receiver]) // 2
    margin = jnp.where((source_of == order[0]) | (receiver == order[0]) | (sizes[receiver] == 0), 0, jnp.maximum(margin, 0))
    passed = jax.random.randint(jax.random.fold_in(own, 4), (number_of // 2,), 0, 1 << 20) % (margin + 1)
    sizes = sizes.at[source_of].add(-passed).at[receiver].add(passed)
    items = jnp.searchsorted(jnp.cumsum(sizes), jnp.arange(rows * top), side="right").astype(jnp.int32)
    grid = items.reshape(top, rows).T
    grid = grid[jax.random.permutation(jax.random.fold_in(own, 1), rows)]
    turn = jax.random.randint(jax.random.fold_in(own, 2), (rows, 1), 0, top)
    return jnp.take_along_axis(grid, (jnp.arange(top)[None, :] + turn) % top, axis=1)


def portions_of(amount, total, reach, lean, full):
    weights = [(1 << 20) // math.isqrt(standing ** lean) + 1 for standing in range(1, amount + 1)]
    largest = reach if full else min(reach, max(-(-total // amount), total * weights[0] // sum(weights)))
    least = 1 if total - largest >= amount - 1 else 0
    counts, spare = [largest] + [least] * (amount - 1), total - largest - least * (amount - 1)
    while spare > 0:
        free = [i for i in range(1, amount) if counts[i] < largest] or [i for i in range(1, amount) if counts[i] < reach]
        mass, remaining = sum([weights[i] for i in free]), spare
        for i in free:
            more = min(reach - counts[i], max(1, remaining * weights[i] // mass), spare)
            counts[i] = counts[i] + more
            spare = spare - more
    return np.array(counts)


def bell_draw(rng, extent, width, reach, cuts=(), held_as=jnp.bfloat16):
    values = jax.random.normal(rng, extent, jnp.float32) * width
    if len(cuts) > 0:
        values = block_levels(rng, extent, cuts, -0.22, 0.18) * values
    return jnp.clip(values, min=-reach, max=reach).astype(held_as)


def setup_inputs(seed: int = 0) -> dict:
    splits = jax.random.split(jax.random.key(seed), 15)
    residual = bell_draw(splits[0], (LENGTH, D), 0.5, 3.0, ((0, 128),))
    queries = draw_queries(jax.random.fold_in(splits[14], 71), 0)
    key_heads = draw_key_heads(jax.random.fold_in(splits[14], 71), 0)
    value_heads = bell_draw(splits[3], (LENGTH, KV_HEADS * HD), 1.0, 6.0, ((0, 16), (1, 8)))
    out_proj = bell_draw(splits[4], (HEADS * HD, D), (GROUP * HD // 2) ** -0.5, 0.3125, ((0, 8), (1, 16)))
    norm_gain = jnp.clip(1.0 + 0.1 * jax.random.normal(splits[5], (D,), jnp.float32), 0.5, 1.5)
    gate_weight = bell_draw(splits[6], (EXPERTS, FF, D), D ** -0.5, 0.078125, ((0, 8), (1, 16)))
    up_weight = bell_draw(splits[7], (EXPERTS, FF, D), D ** -0.5, 0.078125, ((0, 8), (1, 16)))
    down_weight = bell_draw(splits[8], (EXPERTS, FF, D), FF ** -0.5, 0.0625, ((0, 8), (1, 16)))
    adapter_in = bell_draw(splits[9], (EXPERTS, ADAPTERS * RANK, D), D ** -0.5, 0.078125, ((0, 8), (1, 16)))
    adapter_out = bell_draw(splits[10], (EXPERTS, ADAPTERS * RANK, D), (ADAPTERS * RANK) ** -0.5, 0.1875, ((0, 8), (1, 16)))
    route_ids_keys = jax.random.split(jax.random.fold_in(splits[11], 1), LENGTH // TOK_DEV)
    route_ids_turns = jax.random.permutation(jax.random.fold_in(splits[11], 3), LENGTH // TOK_DEV)
    route_ids = jax.vmap(lambda own, number: deal_out(jax.random.fold_in(splits[11], 2), own, number, TOK_DEV, EXPERTS, 2, CAP, 2))(route_ids_keys, route_ids_turns).reshape((LENGTH, 2))
    route_gates = jnp.clip(0.2 + 0.8 * jax.random.uniform(splits[12], (LENGTH, 2), jnp.float32) ** block_levels(splits[12], (LENGTH, 2), ((0, 128),), -0.2, 0.2), 0.2, 1.0)
    adapter_mix = set_ends(jax.random.randint(splits[13], (LENGTH, ADAPTERS), -8, 9), jax.random.fold_in(splits[13], 1), -8, 8).astype(jnp.int32)
    return {"residual": residual, "queries": queries, "key_heads": key_heads, "value_heads": value_heads, "out_proj": out_proj, "norm_gain": norm_gain, "gate_weight": gate_weight, "up_weight": up_weight, "down_weight": down_weight, "adapter_in": adapter_in, "adapter_out": adapter_out, "route_ids": route_ids, "route_gates": route_gates, "adapter_mix": adapter_mix}


def attention_heads(queries, key_heads, value_heads):
    length = queries.shape[0]
    query_stack = queries.reshape(length, HEADS, HD).transpose(1, 0, 2)
    key_stack = key_heads.reshape(length, KV_HEADS, HD).transpose(1, 0, 2)
    value_stack = value_heads.reshape(length, KV_HEADS, HD).transpose(1, 0, 2)
    places = jnp.arange(length)
    allowed = places[None, :] <= places[:, None]
    scaling = HD ** (-0.5)

    def one_head(index):
        kv_index = index // GROUP
        scores = jnp.dot(query_stack[index], key_stack[kv_index].T, preferred_element_type=jnp.float32) * scaling
        scores = jnp.where(allowed, scores, -1e+30)
        highest = lax.optimization_barrier(jnp.max(scores, axis=1, keepdims=True))
        probs = jnp.exp(scores - highest)
        totals = lax.optimization_barrier(jnp.sum(probs, axis=1, keepdims=True))
        summed = jnp.dot(probs.astype(jnp.bfloat16), value_stack[kv_index], preferred_element_type=jnp.float32)
        return (summed / totals).astype(jnp.bfloat16)
    outputs = lax.map(one_head, jnp.arange(HEADS))
    return outputs.transpose(1, 0, 2).reshape(length, HEADS * HD)

def contract_last(left, right):
    return lax.dot_general(left, right, (((1,), (1,)), ((), ())), preferred_element_type=jnp.float32)

def expert_rows(inputs):
    rows, mix_rows, gate_part, up_part, down_part, in_part, out_part = inputs
    gate = contract_last(rows, gate_part)
    upward = contract_last(rows, up_part)
    units = (jax.nn.silu(gate) * upward).astype(jnp.bfloat16)
    scales = jnp.repeat(mix_rows.astype(jnp.float32) / 8.0, RANK, axis=1)
    lowrank = (contract_last(rows, in_part) * scales).astype(jnp.bfloat16)
    result = jnp.dot(units, down_part, preferred_element_type=jnp.float32) + jnp.dot(lowrank, out_part, preferred_element_type=jnp.float32)
    return result.astype(jnp.bfloat16)

def reference(residual, queries, key_heads, value_heads, out_proj, norm_gain, gate_weight, up_weight, down_weight, adapter_in, adapter_out, route_ids, route_gates, adapter_mix):
    attended = attention_heads(queries, key_heads, value_heads)
    projected = lax.optimization_barrier(jnp.dot(attended, out_proj, preferred_element_type=jnp.float32).astype(jnp.bfloat16))
    hidden_state = lax.optimization_barrier((residual.astype(jnp.float32) + projected.astype(jnp.float32)).astype(jnp.bfloat16))
    wide = hidden_state.astype(jnp.float32)
    normed = (wide * lax.rsqrt(lax.optimization_barrier(jnp.mean(wide * wide, axis=1, keepdims=True)) + 1e-05) * norm_gain.astype(jnp.float32)).astype(jnp.bfloat16)
    length = residual.shape[0]
    blocks = length // TOK_DEV
    flat = route_ids.reshape(blocks, 2 * TOK_DEV).astype(jnp.int32)
    onehot = (flat[:, :, None] == jnp.arange(EXPERTS).astype(jnp.int32)[None, None, :]).astype(jnp.int32)
    ranks = lax.optimization_barrier(jnp.sum((jnp.cumsum(onehot, axis=1) - 1) * onehot, axis=2))
    slots = (jnp.arange(blocks).astype(jnp.int32)[:, None] * CAP + ranks).reshape(-1).astype(jnp.int32)
    pair_expert = flat.reshape(-1)
    pair_token = (jnp.arange(2 * length) // 2).astype(jnp.int32)
    table = jnp.zeros((EXPERTS, blocks * CAP), jnp.int32).at[pair_expert, slots].set(pair_token)
    outputs = lax.map(expert_rows, (normed[table], adapter_mix[table], gate_weight, up_weight, down_weight, adapter_in, adapter_out))
    pair_out = lax.optimization_barrier(outputs[pair_expert, slots].reshape(length, 2, -1))
    routed = lax.optimization_barrier(jnp.sum(route_gates.astype(jnp.float32)[:, :, None] * pair_out.astype(jnp.float32), axis=1))
    return (wide + routed).astype(jnp.bfloat16)
```

```python
import functools

import jax
import jax.numpy as jnp
from jax import lax
from jax.experimental import pallas as pl
from jax.experimental.pallas import tpu as pltpu
from jax.sharding import PartitionSpec as P

RANK = 16


MESH = pl.DeviceIdType.MESH
CAP = 5
Z = 4


def dot(left, right):
    return jnp.dot(left, right, preferred_element_type=jnp.float32)


def contract_last(left, right):
    return lax.dot_general(
        left, right, (((1,), (1,)), ((), ())), preferred_element_type=jnp.float32
    )


def tile_of(size, most):
    while size % most:
        most -= 128
    return most


def place_on_mesh():
    me = lax.axis_index("seq")
    core = lax.rem(me, 2)
    x_hi = lax.rem(me // 2, 2)
    z = me // 4
    return me, z, x_hi, core


def seq_of(z, x_hi, core):
    return lax.rem(z + Z, Z) * 4 + x_hi * 2 + core


def expert_kernel(
    exps,
    disp,
    hidden,
    slot_gates,
    gate_hbm,
    up_hbm,
    down_hbm,
    in_hbm,
    out_hbm,
    out,
    arrived,
    wide_slots,
    rows,
    w_first,
    w_second,
    units,
    pair_send,
    pair_recv,
    own,
    z_send,
    half_low,
    half_high,
    full_low,
    full_high,
    x_send,
    x_recv,
    back,
    back_wide,
    returned,
    returned_wide,
    weight_sems,
    disp_send,
    disp_recv,
    ring_send,
    ring_recv,
    pass_send,
    pass_recv,
    pair_send_sem,
    pair_recv_sem,
    z_send_sem,
    z_recv_sem,
    x_send_sem,
    x_recv_sem,
    back_send,
    back_recv,
    local_sem,
):
    bf16, f32 = jnp.bfloat16, jnp.float32
    width = hidden.shape[1]
    half = width // 2
    quarter = half // 2
    lanes = half // 128
    slot_rows = disp.shape[3]
    hidden_units = gate_hbm.shape[0]
    adapters = in_hbm.shape[0]
    block = 2 * exps * CAP
    many = 4 * block
    peers = 2 * exps

    me, z, x_hi, core = place_on_mesh()
    exp = lax.axis_index("exp")
    sibling = (seq_of(z, x_hi, 1 - core), exp)
    above = (seq_of(z + 1, x_hi, core), exp)
    below = (seq_of(z - 1, x_hi, core), exp)
    across = (seq_of(z, 1 - x_hi, core), exp)
    mine = core * exps + exp

    def peer(step):
        at = lax.rem(mine + step, peers)
        return at, (seq_of(z, x_hi, at // exps), lax.rem(at, exps))

    barrier = pltpu.get_barrier_semaphore()

    def greet(step, carry):
        pl.semaphore_signal(barrier, inc=1, device_id=peer(step)[1], device_id_type=MESH)
        return carry

    lax.fori_loop(1, peers, greet, 0)
    for other in (above, below, across):
        pl.semaphore_signal(barrier, inc=1, device_id=other, device_id_type=MESH)

    loads = []
    for side in range(2):
        columns = pl.ds(side * half, half)
        for source, place, start in (
            (gate_hbm, w_first, 0),
            (up_hbm, w_first, hidden_units),
            (in_hbm, w_first, 2 * hidden_units),
            (down_hbm, w_second, 0),
            (out_hbm, w_second, hidden_units),
        ):
            load = pltpu.make_async_copy(
                source.at[:, columns],
                place.at[side, pl.ds(start, source.shape[0]), :],
                weight_sems.at[len(loads)],
            )
            load.start()
            loads.append(load)

    pl.semaphore_wait(barrier, peers - 1 + 3)

    def remote(source, target, send, recv, device):
        return pltpu.make_async_remote_copy(
            src_ref=source,
            dst_ref=target,
            send_sem=send,
            recv_sem=recv,
            device_id=device,
            device_id_type=MESH,
        )

    def dispatch(step):
        at, device = peer(step)
        return remote(
            disp.at[at // exps, lax.rem(at, exps)],
            arrived.at[mine],
            disp_send.at[step],
            disp_recv.at[step],
            device,
        )

    def dispatch_start(step, carry):
        dispatch(step).start()
        return carry

    def dispatch_wait(step, carry):
        dispatch(step).wait()
        return carry

    lax.fori_loop(1, peers, dispatch_start, 0)
    keep = pltpu.make_async_copy(disp.at[core, exp], arrived.at[mine], local_sem)
    keep.start()
    keep.wait()
    lax.fori_loop(1, peers, dispatch_wait, 0)
    wide_slots[...] = arrived[...].astype(f32).reshape(block * slot_rows, 128)
    for lane in range(lanes + 1):
        rows[core, 0:block, lane * 128 : (lane + 1) * 128] = wide_slots[
            pl.ds(lane, block, stride=slot_rows), :
        ].astype(bf16)

    all_columns = pl.ds(0, half + 128)
    cut = (lanes + 2) // 2 * 128
    first_columns, last_columns = pl.ds(0, cut), pl.ds(cut, half + 128 - cut)

    def part(place, columns=all_columns):
        return rows.at[core, pl.ds(place * block, block), columns]

    started = []

    def begin(copy):
        copy.start()
        started.append(copy)
        return copy

    def hand_over(place):
        return begin(
            remote(part(place), part(place), pass_send.at[place], pass_recv.at[place], sibling)
        )

    def hop(index, source, target, device, columns=all_columns):
        return begin(
            remote(
                part(source, columns),
                part(target, columns),
                ring_send.at[index],
                ring_recv.at[index],
                device,
            )
        )

    handed = {}
    up_0 = hop(0, 0, 1, above)
    down_0 = hop(1, 0, 2, below)
    cross = hop(2, 0, 4, across)
    handed[0] = hand_over(0)
    up_0.wait_recv()
    up_1 = hop(3, 1, 3, above, first_columns)
    handed[1] = hand_over(1)
    down_0.wait_recv()
    down_1 = hop(4, 2, 3, below, last_columns)
    handed[2] = hand_over(2)
    cross.wait_recv()
    up_2 = hop(5, 4, 5, above)
    down_2 = hop(6, 4, 6, below)
    handed[4] = hand_over(4)
    up_1.wait_recv()
    down_1.wait_recv()
    handed[3] = hand_over(3)
    for load in loads:
        load.wait()

    unit_tile = tile_of(hidden_units, 256)
    mix_width = 64
    adapter_at = lax.broadcasted_iota(jnp.int32, (mix_width, adapters), 1) // RANK
    spread = (
        lax.broadcasted_iota(jnp.int32, (mix_width, adapters), 0)
        == adapter_at + me * (adapters // RANK)
    ).astype(bf16)

    def first_layer(group):
        at = pl.ds(group * many, many)

        def project(start, size):
            return contract_last(
                rows[0, at, 0:half], w_first[0, pl.ds(start, size), :]
            ) + contract_last(rows[1, at, 0:half], w_first[1, pl.ds(start, size), :])

        def tile(index, carry):
            start = pl.multiple_of(index * unit_tile, unit_tile)
            gate = project(start, unit_tile)
            upward = project(hidden_units + start, unit_tile)
            units[:, pl.ds(start, unit_tile)] = (jax.nn.silu(gate) * upward).astype(bf16)
            return carry

        lax.fori_loop(0, hidden_units // unit_tile, tile, 0)
        scales = dot(rows[0, at, half : half + mix_width], spread) / 8.0
        units[:, hidden_units : hidden_units + adapters] = (
            project(2 * hidden_units, adapters) * scales
        ).astype(bf16)

    out_tile = tile_of(quarter, 512)

    def second_layer(group, side, part_of, target):
        def tile(index, carry):
            start = pl.multiple_of(part_of * quarter + index * out_tile, 128)
            value = dot(units[...], w_second[side, :, pl.ds(start, out_tile)])
            target[group, :, pl.ds(start, out_tile)] = value.astype(target.dtype)
            return carry

        lax.fori_loop(0, quarter // out_tile, tile, 0)

    quarters = [pl.ds(0, quarter), pl.ds(quarter, quarter)]

    def swap(group, part_of):
        index = group * 2 + part_of
        return begin(
            remote(
                pair_send.at[group, :, quarters[part_of]],
                pair_recv.at[group, :, quarters[part_of]],
                pair_send_sem.at[index],
                pair_recv_sem.at[index],
                sibling,
            )
        )

    def z_copy(group, index, source, target, device):
        at = group * 6 + index
        return begin(remote(source, target, z_send_sem.at[at], z_recv_sem.at[at], device))

    def pair_sum(group, place, part_of):
        at = pl.ds(place * block, block)
        return own[group, at, quarters[part_of]] + pair_recv[
            group, at, quarters[part_of]
        ].astype(f32)

    def reduce_first(group, swapped, flows):
        swapped[0].wait_recv()
        z_send[group, 2, :, quarters[0]] = pair_sum(group, 3, 0).astype(bf16)
        flows["half_low"] = z_copy(
            group, 0, z_send.at[group, 2, :, quarters[0]], half_low.at[group], above
        )
        z_send[group, 0, :, quarters[0]] = pair_sum(group, 1, 0).astype(bf16)
        flows["high_0"] = z_copy(
            group,
            1,
            z_send.at[group, 0, :, quarters[0]],
            full_high.at[group, :, quarters[0]],
            below,
        )
        own[group, 0:block, quarters[0]] = pair_sum(group, 0, 0)
        own[group, 2 * block : 3 * block, quarters[0]] = pair_sum(group, 2, 0)

    def reduce_second(group, swapped, flows):
        swapped[1].wait_recv()
        z_send[group, 2, :, quarters[1]] = pair_sum(group, 3, 1).astype(bf16)
        flows["half_high"] = z_copy(
            group, 2, z_send.at[group, 2, :, quarters[1]], half_high.at[group], below
        )
        z_send[group, 1, :, quarters[1]] = pair_sum(group, 2, 1).astype(bf16)
        flows["low_1"] = z_copy(
            group,
            3,
            z_send.at[group, 1, :, quarters[1]],
            full_low.at[group, :, quarters[1]],
            above,
        )
        own[group, 0:block, quarters[1]] = pair_sum(group, 0, 1)
        own[group, block : 2 * block, quarters[1]] = pair_sum(group, 1, 1)

    def pass_on(group, flows):
        flows["half_low"].wait_recv()
        z_send[group, 1, :, quarters[0]] = (
            own[group, 2 * block : 3 * block, quarters[0]] + half_low[group].astype(f32)
        ).astype(bf16)
        flows["low_0"] = z_copy(
            group,
            4,
            z_send.at[group, 1, :, quarters[0]],
            full_low.at[group, :, quarters[0]],
            above,
        )
        flows["half_high"].wait_recv()
        z_send[group, 0, :, quarters[1]] = (
            own[group, block : 2 * block, quarters[1]] + half_high[group].astype(f32)
        ).astype(bf16)
        flows["high_1"] = z_copy(
            group,
            5,
            z_send.at[group, 0, :, quarters[1]],
            full_high.at[group, :, quarters[1]],
            below,
        )

    def settled(group, part_of, flows):
        flows[f"low_{part_of}"].wait_recv()
        flows[f"high_{part_of}"].wait_recv()
        return (
            own[group, 0:block, quarters[part_of]]
            + full_low[group, :, quarters[part_of]].astype(f32)
            + full_high[group, :, quarters[part_of]].astype(f32)
        )

    flows = ({}, {})
    for place in range(4):
        handed[place].wait_recv()
    first_layer(0)
    up_2.wait_recv()
    up_3 = hop(7, 5, 7, above, first_columns)
    handed[5] = hand_over(5)
    down_2.wait_recv()
    down_3 = hop(8, 6, 7, below, last_columns)
    handed[6] = hand_over(6)
    second_layer(0, 1 - core, 0, pair_send)
    swap_0 = [swap(0, 0)]
    second_layer(0, 1 - core, 1, pair_send)
    swap_0.append(swap(0, 1))
    second_layer(0, core, 0, own)
    reduce_first(0, swap_0, flows[0])
    second_layer(0, core, 1, own)
    reduce_second(0, swap_0, flows[0])
    up_3.wait_recv()
    down_3.wait_recv()
    handed[7] = hand_over(7)
    for place in range(4, 8):
        handed[place].wait_recv()
    first_layer(1)
    pass_on(0, flows[0])
    second_layer(1, 1 - core, 0, pair_send)
    swap_1 = [swap(1, 0)]
    second_layer(1, 1 - core, 1, pair_send)
    swap_1.append(swap(1, 1))
    second_layer(1, core, 0, own)
    reduce_first(1, swap_1, flows[1])
    second_layer(1, core, 1, own)
    reduce_second(1, swap_1, flows[1])
    pass_on(1, flows[1])
    crossing = []
    for part_of in range(2):
        own[0, 0:block, quarters[part_of]] = settled(0, part_of, flows[0])
    for part_of in (1, 0):
        x_send[:, quarters[part_of]] = settled(1, part_of, flows[1]).astype(bf16)
        crossing.append(
            begin(
                remote(
                    x_send.at[:, quarters[part_of]],
                    x_recv.at[:, quarters[part_of]],
                    x_send_sem.at[part_of],
                    x_recv_sem.at[part_of],
                    across,
                )
            )
        )
    for copy in crossing:
        copy.wait_recv()
    for lane in range(lanes):
        columns = slice(lane * 128, (lane + 1) * 128)
        back_wide[pl.ds(lane, block, stride=lanes), :] = own[0, 0:block, columns] + x_recv[
            :, columns
        ].astype(f32)
    back[...] = back_wide[...].reshape(back.shape).astype(bf16)

    def give_back(step):
        at, device = peer(step)
        return remote(
            back.at[at], returned.at[core, exp], back_send.at[step], back_recv.at[step], device
        )

    def give_start(step, carry):
        give_back(step).start()
        return carry

    def give_wait(step, carry):
        give_back(step).wait()
        return carry

    lax.fori_loop(1, peers, give_start, 0)
    keep = pltpu.make_async_copy(back.at[mine], returned.at[core, exp], local_sem)
    keep.start()
    keep.wait()
    for copy in started:
        copy.wait_send()
    lax.fori_loop(1, peers, give_wait, 0)

    slots = exps * CAP
    returned_wide[...] = returned[...].astype(f32).reshape(2 * slots * lanes, 128)
    gates = slot_gates[...]
    for side in range(2):
        for lane in range(lanes):
            columns = slice(side * half + lane * 128, side * half + (lane + 1) * 128)
            values = returned_wide[pl.ds(side * slots * lanes + lane, slots, stride=lanes), :]
            routed = jnp.dot(
                gates, values, precision=lax.Precision.HIGHEST, preferred_element_type=f32
            )
            out[:, columns] = (hidden[:, columns].astype(f32) + routed).astype(bf16)


def expert_layer(disp, hidden, slot_gates, gate, up, down, adapter_in, adapter_out):
    bf16, f32 = jnp.bfloat16, jnp.float32
    exps = disp.shape[1]
    tokens, width = hidden.shape
    half = width // 2
    lanes = half // 128
    slot_rows = disp.shape[3]
    block = 2 * exps * CAP
    hidden_units, adapters = gate.shape[0], adapter_in.shape[0]
    inner = hidden_units + adapters
    dma = pltpu.SemaphoreType.DMA
    vmem = pl.BlockSpec(memory_space=pltpu.VMEM)
    anywhere = pl.BlockSpec(memory_space=pl.ANY)
    return pl.pallas_call(
        functools.partial(expert_kernel, exps),
        out_shape=jax.ShapeDtypeStruct((tokens, width), bf16),
        in_specs=[vmem] * 3 + [anywhere] * 5,
        out_specs=vmem,
        scratch_shapes=[
            pltpu.VMEM((2 * exps, CAP, slot_rows, 128), bf16),
            pltpu.VMEM((block * slot_rows, 128), f32),
            pltpu.VMEM((2, 8 * block, half + 128), bf16),
            pltpu.VMEM((2, hidden_units + inner, half), bf16),
            pltpu.VMEM((2, inner, half), bf16),
            pltpu.VMEM((4 * block, inner), bf16),
            pltpu.VMEM((2, 4 * block, half), bf16),
            pltpu.VMEM((2, 4 * block, half), bf16),
            pltpu.VMEM((2, 4 * block, half), f32),
            pltpu.VMEM((2, 3, block, half), bf16),
            pltpu.VMEM((2, block, half // 2), bf16),
            pltpu.VMEM((2, block, half // 2), bf16),
            pltpu.VMEM((2, block, half), bf16),
            pltpu.VMEM((2, block, half), bf16),
            pltpu.VMEM((block, half), bf16),
            pltpu.VMEM((block, half), bf16),
            pltpu.VMEM((2 * exps, CAP, lanes, 128), bf16),
            pltpu.VMEM((block * lanes, 128), f32),
            pltpu.VMEM((2, exps, CAP, lanes, 128), bf16),
            pltpu.VMEM((2 * exps * CAP * lanes, 128), f32),
            dma((10,)),
            dma((2 * exps,)),
            dma((2 * exps,)),
            dma((9,)),
            dma((9,)),
            dma((8,)),
            dma((8,)),
            dma((4,)),
            dma((4,)),
            dma((12,)),
            dma((12,)),
            dma((2,)),
            dma((2,)),
            dma((2 * exps,)),
            dma((2 * exps,)),
            dma,
        ],
        compiler_params=pltpu.CompilerParams(
            collective_id=1, has_side_effects=True, vmem_limit_bytes=62 * 2**20
        ),
    )(disp, hidden, slot_gates, gate, up, down, adapter_in, adapter_out)


def rounded(value):
    return lax.optimization_barrier(value.astype(jnp.bfloat16))


def on_device(
    residual,
    queries,
    key_heads,
    value_heads,
    out_proj,
    norm_gain,
    gate_weight,
    up_weight,
    down_weight,
    adapter_in,
    adapter_out,
    route_ids,
    route_gates,
    adapter_mix,
):
    seq_count = lax.axis_size("seq")
    group_count = lax.axis_size("exp")
    seq_index = lax.axis_index("seq")
    seq_rows = queries.shape[0]
    head_width = value_heads.shape[1]
    group = queries.shape[1] // head_width
    query_blocks = queries.reshape(seq_rows, group, head_width)
    query_place = seq_index * seq_rows + jnp.arange(seq_rows, dtype=jnp.int32)
    scaling = head_width ** (-0.5)
    running_max = jnp.full((group, seq_rows), -1e30, jnp.float32)
    key_piece = lax.all_gather(key_heads, "seq", axis=0, tiled=True)
    value_piece = lax.all_gather(value_heads, "seq", axis=0, tiled=True)
    key_place = jnp.arange(key_piece.shape[0], dtype=jnp.int32)
    allowed = key_place[None, None, :] <= query_place[None, :, None]
    scores = (
        jnp.einsum("rgd,kd->grk", query_blocks, key_piece, preferred_element_type=jnp.float32)
        * scaling
    )
    scores = jnp.where(allowed, scores, -1e30)
    new_max = jnp.maximum(running_max, jnp.max(scores, axis=2))
    probs = jnp.where(allowed, jnp.exp(scores - new_max[:, :, None]), 0.0)
    running_sum = jnp.sum(probs, axis=2)
    update = jnp.einsum(
        "grk,kd->grd", probs.astype(jnp.bfloat16), value_piece, preferred_element_type=jnp.float32
    )
    attended = (
        (update / running_sum[:, :, None])
        .astype(jnp.bfloat16)
        .transpose(1, 0, 2)
        .reshape(seq_rows, group * head_width)
    )
    tok_rows = residual.shape[0]
    full_rows = jnp.dot(
        attended,
        lax.all_gather(out_proj, "seq", axis=1, tiled=True),
        preferred_element_type=jnp.float32,
    )
    projected = rounded(
        lax.psum_scatter(
            full_rows.astype(jnp.bfloat16), "exp", scatter_dimension=0, tiled=True
        ).astype(jnp.float32)
    )
    hidden_state = rounded(residual.astype(jnp.float32) + projected.astype(jnp.float32))
    wide = hidden_state.astype(jnp.float32)
    normed = (
        wide * lax.rsqrt(jnp.mean(wide * wide, axis=1, keepdims=True) + 1e-05) * norm_gain
    ).astype(jnp.bfloat16)
    capacity = max(tok_rows * 5 // 16, 2 * tok_rows // group_count)
    pair_expert = route_ids.reshape(-1)
    expert_ids = jnp.arange(group_count, dtype=jnp.int32)
    onehot = (pair_expert[:, None] == expert_ids[None, :]).astype(jnp.int32)
    ranks = jnp.sum((jnp.cumsum(onehot, axis=0) - 1) * onehot, axis=1)
    target = pair_expert * capacity + ranks
    slot_ids = jnp.arange(group_count * capacity, dtype=jnp.int32)
    pair_hit = target[None, :] == slot_ids[:, None]
    pair_token = jnp.arange(2 * tok_rows, dtype=jnp.int32) // 2
    token_ids = jnp.arange(tok_rows, dtype=jnp.int32)
    pair_of_token = (pair_token[:, None] == token_ids[None, :]).astype(jnp.float32)
    placing = jnp.dot(pair_hit.astype(jnp.float32), pair_of_token).astype(jnp.bfloat16)
    send_rows = (
        jnp.dot(placing, normed, preferred_element_type=jnp.float32)
        .astype(jnp.bfloat16)
        .reshape(group_count, capacity, 2, -1, 128)
        .transpose(2, 0, 1, 3, 4)
    )
    send_mix = jnp.dot(
        placing, adapter_mix.astype(jnp.bfloat16), preferred_element_type=jnp.float32
    ).astype(jnp.bfloat16)
    tail = jnp.pad(
        send_mix.reshape(group_count, capacity, 1, -1),
        ((0, 0), (0, 0), (0, 7), (0, 128 - send_mix.shape[1])),
    )
    disp = jnp.concatenate([send_rows, jnp.broadcast_to(tail, (2,) + tail.shape)], axis=3)
    gate_flat = route_gates.reshape(-1)
    weighted = jnp.where(pair_hit, gate_flat[None, :], 0.0)
    slot_gates = jnp.dot(weighted, pair_of_token, precision=lax.Precision.HIGHEST)
    return expert_layer(
        disp,
        hidden_state,
        slot_gates.T,
        gate_weight[0],
        up_weight[0],
        down_weight[0],
        adapter_in[0],
        adapter_out[0],
    )


def solution(mesh):
    in_specs = (
        P(("seq", "exp"), None),
        P("seq", "exp"),
        P("seq", "exp"),
        P("seq", "exp"),
        P("exp", "seq"),
        P(),
        P("exp", "seq", None),
        P("exp", "seq", None),
        P("exp", "seq", None),
        P("exp", "seq", None),
        P("exp", "seq", None),
        P(("seq", "exp"), None),
        P(("seq", "exp"), None),
        P(("seq", "exp"), None),
    )
    out_specs = P(("seq", "exp"), None)
    return jax.shard_map(
        on_device, mesh=mesh, in_specs=in_specs, out_specs=out_specs, check_vma=False
    )
```

```python
import functools

import jax
import jax.numpy as jnp
from jax import lax
from jax.experimental import pallas as pl
from jax.experimental.pallas import tpu as pltpu
from jax.sharding import PartitionSpec as P

RANK = 16


MESH = pl.DeviceIdType.MESH
CAP = 5
Z = 4


def dot(left, right):
    return jnp.dot(left, right, preferred_element_type=jnp.float32)


def contract_last(left, right):
    return lax.dot_general(
        left, right, (((1,), (1,)), ((), ())), preferred_element_type=jnp.float32
    )


def tile_of(size, most):
    while size % most:
        most -= 128
    return most


def place_on_mesh():
    me = lax.axis_index("seq")
    core = lax.rem(me, 2)
    x_hi = lax.rem(me // 2, 2)
    z = me // 4
    return me, z, x_hi, core


def seq_of(z, x_hi, core):
    return lax.rem(z + Z, Z) * 4 + x_hi * 2 + core


def expert_kernel(
    exps,
    disp,
    hidden,
    slot_gates,
    gate_hbm,
    up_hbm,
    down_hbm,
    in_hbm,
    out_hbm,
    out,
    arrived,
    wide_slots,
    rows,
    w_first,
    w_second,
    units,
    pair_send,
    pair_recv,
    own,
    z_send,
    half_low,
    half_high,
    full_low,
    full_high,
    x_send,
    x_recv,
    back,
    back_wide,
    returned,
    returned_wide,
    weight_sems,
    disp_send,
    disp_recv,
    ring_send,
    ring_recv,
    pass_send,
    pass_recv,
    pair_send_sem,
    pair_recv_sem,
    z_send_sem,
    z_recv_sem,
    x_send_sem,
    x_recv_sem,
    back_send,
    back_recv,
    local_sem,
):
    bf16, f32 = jnp.bfloat16, jnp.float32
    width = hidden.shape[1]
    half = width // 2
    quarter = half // 2
    lanes = half // 128
    slot_rows = disp.shape[3]
    hidden_units = gate_hbm.shape[0]
    adapters = in_hbm.shape[0]
    block = 2 * exps * CAP
    many = 4 * block
    peers = 2 * exps

    me, z, x_hi, core = place_on_mesh()
    exp = lax.axis_index("exp")
    sibling = (seq_of(z, x_hi, 1 - core), exp)
    above = (seq_of(z + 1, x_hi, core), exp)
    below = (seq_of(z - 1, x_hi, core), exp)
    across = (seq_of(z, 1 - x_hi, core), exp)
    mine = core * exps + exp

    def peer(step):
        at = lax.rem(mine + step, peers)
        return at, (seq_of(z, x_hi, at // exps), lax.rem(at, exps))

    barrier = pltpu.get_barrier_semaphore()

    def greet(step, carry):
        pl.semaphore_signal(barrier, inc=1, device_id=peer(step)[1], device_id_type=MESH)
        return carry

    lax.fori_loop(1, peers, greet, 0)
    for other in (above, below, across):
        pl.semaphore_signal(barrier, inc=1, device_id=other, device_id_type=MESH)

    loads = []
    for side in range(2):
        columns = pl.ds(side * half, half)
        for source, place, start in (
            (gate_hbm, w_first, 0),
            (up_hbm, w_first, hidden_units),
            (in_hbm, w_first, 2 * hidden_units),
            (down_hbm, w_second, 0),
            (out_hbm, w_second, hidden_units),
        ):
            load = pltpu.make_async_copy(
                source.at[:, columns],
                place.at[side, pl.ds(start, source.shape[0]), :],
                weight_sems.at[len(loads)],
            )
            load.start()
            loads.append(load)

    pl.semaphore_wait(barrier, peers - 1 + 3)

    def remote(source, target, send, recv, device):
        return pltpu.make_async_remote_copy(
            src_ref=source,
            dst_ref=target,
            send_sem=send,
            recv_sem=recv,
            device_id=device,
            device_id_type=MESH,
        )

    def dispatch(step):
        at, device = peer(step)
        return remote(
            disp.at[at // exps, lax.rem(at, exps)],
            arrived.at[mine],
            disp_send.at[step],
            disp_recv.at[step],
            device,
        )

    def dispatch_start(step, carry):
        dispatch(step).start()
        return carry

    def dispatch_wait(step, carry):
        dispatch(step).wait()
        return carry

    lax.fori_loop(1, peers, dispatch_start, 0)
    keep = pltpu.make_async_copy(disp.at[core, exp], arrived.at[mine], local_sem)
    keep.start()
    keep.wait()
    lax.fori_loop(1, peers, dispatch_wait, 0)
    wide_slots[...] = arrived[...].astype(f32).reshape(block * slot_rows, 128)
    for lane in range(lanes + 1):
        rows[core, 0:block, lane * 128 : (lane + 1) * 128] = wide_slots[
            pl.ds(lane, block, stride=slot_rows), :
        ].astype(bf16)

    all_columns = pl.ds(0, half + 128)
    cut = (lanes + 2) // 2 * 128
    first_columns, last_columns = pl.ds(0, cut), pl.ds(cut, half + 128 - cut)

    def part(place, columns=all_columns):
        return rows.at[core, pl.ds(place * block, block), columns]

    started = []

    def begin(copy):
        copy.start()
        started.append(copy)
        return copy

    def hand_over(place):
        return begin(
            remote(part(place), part(place), pass_send.at[place], pass_recv.at[place], sibling)
        )

    def hop(index, source, target, device, columns=all_columns):
        return begin(
            remote(
                part(source, columns),
                part(target, columns),
                ring_send.at[index],
                ring_recv.at[index],
                device,
            )
        )

    handed = {}
    up_0 = hop(0, 0, 1, above)
    down_0 = hop(1, 0, 2, below)
    cross = hop(2, 0, 4, across)
    handed[0] = hand_over(0)
    up_0.wait_recv()
    up_1 = hop(3, 1, 3, above, first_columns)
    handed[1] = hand_over(1)
    down_0.wait_recv()
    down_1 = hop(4, 2, 3, below, last_columns)
    handed[2] = hand_over(2)
    cross.wait_recv()
    up_2 = hop(5, 4, 5, above)
    down_2 = hop(6, 4, 6, below)
    handed[4] = hand_over(4)
    up_1.wait_recv()
    down_1.wait_recv()
    handed[3] = hand_over(3)
    for load in loads:
        load.wait()

    unit_tile = tile_of(hidden_units, 256)
    mix_width = 64
    adapter_at = lax.broadcasted_iota(jnp.int32, (mix_width, adapters), 1) // RANK
    spread = (
        lax.broadcasted_iota(jnp.int32, (mix_width, adapters), 0)
        == adapter_at + me * (adapters // RANK)
    ).astype(bf16)

    def first_layer(group):
        at = pl.ds(group * many, many)

        def project(start, size):
            return contract_last(
                rows[0, at, 0:half], w_first[0, pl.ds(start, size), :]
            ) + contract_last(rows[1, at, 0:half], w_first[1, pl.ds(start, size), :])

        def tile(index, carry):
            start = pl.multiple_of(index * unit_tile, unit_tile)
            gate = project(start, unit_tile)
            upward = project(hidden_units + start, unit_tile)
            units[:, pl.ds(start, unit_tile)] = (jax.nn.silu(gate) * upward).astype(bf16)
            return carry

        lax.fori_loop(0, hidden_units // unit_tile, tile, 0)
        scales = dot(rows[0, at, half : half + mix_width], spread) / 8.0
        units[:, hidden_units : hidden_units + adapters] = (
            project(2 * hidden_units, adapters) * scales
        ).astype(bf16)

    out_tile = tile_of(quarter, 512)

    def second_layer(group, side, part_of, target):
        def tile(index, carry):
            start = pl.multiple_of(part_of * quarter + index * out_tile, 128)
            value = dot(units[...], w_second[side, :, pl.ds(start, out_tile)])
            target[group, :, pl.ds(start, out_tile)] = value.astype(target.dtype)
            return carry

        lax.fori_loop(0, quarter // out_tile, tile, 0)

    quarters = [pl.ds(0, quarter), pl.ds(quarter, quarter)]

    def swap(group, part_of):
        index = group * 2 + part_of
        return begin(
            remote(
                pair_send.at[group, :, quarters[part_of]],
                pair_recv.at[group, :, quarters[part_of]],
                pair_send_sem.at[index],
                pair_recv_sem.at[index],
                sibling,
            )
        )

    def z_copy(group, index, source, target, device):
        at = group * 6 + index
        return begin(remote(source, target, z_send_sem.at[at], z_recv_sem.at[at], device))

    def pair_sum(group, place, part_of):
        at = pl.ds(place * block, block)
        return own[group, at, quarters[part_of]] + pair_recv[
            group, at, quarters[part_of]
        ].astype(f32)

    def reduce_first(group, swapped, flows):
        swapped[0].wait_recv()
        z_send[group, 2, :, quarters[0]] = pair_sum(group, 3, 0).astype(bf16)
        flows["half_low"] = z_copy(
            group, 0, z_send.at[group, 2, :, quarters[0]], half_low.at[group], above
        )
        z_send[group, 0, :, quarters[0]] = pair_sum(group, 1, 0).astype(bf16)
        flows["high_0"] = z_copy(
            group,
            1,
            z_send.at[group, 0, :, quarters[0]],
            full_high.at[group, :, quarters[0]],
            below,
        )
        own[group, 0:block, quarters[0]] = pair_sum(group, 0, 0)
        own[group, 2 * block : 3 * block, quarters[0]] = pair_sum(group, 2, 0)

    def reduce_second(group, swapped, flows):
        swapped[1].wait_recv()
        z_send[group, 2, :, quarters[1]] = pair_sum(group, 3, 1).astype(bf16)
        flows["half_high"] = z_copy(
            group, 2, z_send.at[group, 2, :, quarters[1]], half_high.at[group], below
        )
        z_send[group, 1, :, quarters[1]] = pair_sum(group, 2, 1).astype(bf16)
        flows["low_1"] = z_copy(
            group,
            3,
            z_send.at[group, 1, :, quarters[1]],
            full_low.at[group, :, quarters[1]],
            above,
        )
        own[group, 0:block, quarters[1]] = pair_sum(group, 0, 1)
        own[group, block : 2 * block, quarters[1]] = pair_sum(group, 1, 1)

    def pass_on(group, flows):
        flows["half_low"].wait_recv()
        z_send[group, 1, :, quarters[0]] = (
            own[group, 2 * block : 3 * block, quarters[0]] + half_low[group].astype(f32)
        ).astype(bf16)
        flows["low_0"] = z_copy(
            group,
            4,
            z_send.at[group, 1, :, quarters[0]],
            full_low.at[group, :, quarters[0]],
            above,
        )
        flows["half_high"].wait_recv()
        z_send[group, 0, :, quarters[1]] = (
            own[group, block : 2 * block, quarters[1]] + half_high[group].astype(f32)
        ).astype(bf16)
        flows["high_1"] = z_copy(
            group,
            5,
            z_send.at[group, 0, :, quarters[1]],
            full_high.at[group, :, quarters[1]],
            below,
        )

    def settled(group, part_of, flows):
        flows[f"low_{part_of}"].wait_recv()
        flows[f"high_{part_of}"].wait_recv()
        return (
            own[group, 0:block, quarters[part_of]]
            + full_low[group, :, quarters[part_of]].astype(f32)
            + full_high[group, :, quarters[part_of]].astype(f32)
        )

    flows = ({}, {})
    for place in range(4):
        handed[place].wait_recv()
    first_layer(0)
    up_2.wait_recv()
    up_3 = hop(7, 5, 7, above, first_columns)
    handed[5] = hand_over(5)
    down_2.wait_recv()
    down_3 = hop(8, 6, 7, below, last_columns)
    handed[6] = hand_over(6)
    second_layer(0, 1 - core, 0, pair_send)
    swap_0 = [swap(0, 0)]
    second_layer(0, 1 - core, 1, pair_send)
    swap_0.append(swap(0, 1))
    second_layer(0, core, 0, own)
    reduce_first(0, swap_0, flows[0])
    second_layer(0, core, 1, own)
    reduce_second(0, swap_0, flows[0])
    up_3.wait_recv()
    down_3.wait_recv()
    handed[7] = hand_over(7)
    for place in range(4, 8):
        handed[place].wait_recv()
    first_layer(1)
    pass_on(0, flows[0])
    second_layer(1, 1 - core, 0, pair_send)
    swap_1 = [swap(1, 0)]
    second_layer(1, 1 - core, 1, pair_send)
    swap_1.append(swap(1, 1))
    second_layer(1, core, 0, own)
    reduce_first(1, swap_1, flows[1])
    second_layer(1, core, 1, own)
    reduce_second(1, swap_1, flows[1])
    pass_on(1, flows[1])
    crossing = []
    for part_of in range(2):
        own[0, 0:block, quarters[part_of]] = settled(0, part_of, flows[0])
    for part_of in (1, 0):
        x_send[:, quarters[part_of]] = settled(1, part_of, flows[1]).astype(bf16)
        crossing.append(
            begin(
                remote(
                    x_send.at[:, quarters[part_of]],
                    x_recv.at[:, quarters[part_of]],
                    x_send_sem.at[part_of],
                    x_recv_sem.at[part_of],
                    across,
                )
            )
        )
    for copy in crossing:
        copy.wait_recv()
    for lane in range(lanes):
        columns = slice(lane * 128, (lane + 1) * 128)
        back_wide[pl.ds(lane, block, stride=lanes), :] = own[0, 0:block, columns] + x_recv[
            :, columns
        ].astype(f32)
    back[...] = back_wide[...].reshape(back.shape).astype(bf16)

    def give_back(step):
        at, device = peer(step)
        return remote(
            back.at[at], returned.at[core, exp], back_send.at[step], back_recv.at[step], device
        )

    def give_start(step, carry):
        give_back(step).start()
        return carry

    def give_wait(step, carry):
        give_back(step).wait()
        return carry

    lax.fori_loop(1, peers, give_start, 0)
    keep = pltpu.make_async_copy(back.at[mine], returned.at[core, exp], local_sem)
    keep.start()
    keep.wait()
    for copy in started:
        copy.wait_send()
    lax.fori_loop(1, peers, give_wait, 0)

    slots = exps * CAP
    returned_wide[...] = returned[...].astype(f32).reshape(2 * slots * lanes, 128)
    gates = slot_gates[...]
    for side in range(2):
        for lane in range(lanes):
            columns = slice(side * half + lane * 128, side * half + (lane + 1) * 128)
            values = returned_wide[pl.ds(side * slots * lanes + lane, slots, stride=lanes), :]
            routed = jnp.dot(
                gates, values, precision=lax.Precision.HIGHEST, preferred_element_type=f32
            )
            out[:, columns] = (hidden[:, columns].astype(f32) + routed).astype(bf16)


def expert_layer(disp, hidden, slot_gates, gate, up, down, adapter_in, adapter_out):
    bf16, f32 = jnp.bfloat16, jnp.float32
    exps = disp.shape[1]
    tokens, width = hidden.shape
    half = width // 2
    lanes = half // 128
    slot_rows = disp.shape[3]
    block = 2 * exps * CAP
    hidden_units, adapters = gate.shape[0], adapter_in.shape[0]
    inner = hidden_units + adapters
    dma = pltpu.SemaphoreType.DMA
    vmem = pl.BlockSpec(memory_space=pltpu.VMEM)
    anywhere = pl.BlockSpec(memory_space=pl.ANY)
    return pl.pallas_call(
        functools.partial(expert_kernel, exps),
        out_shape=jax.ShapeDtypeStruct((tokens, width), bf16),
        in_specs=[vmem] * 3 + [anywhere] * 5,
        out_specs=vmem,
        scratch_shapes=[
            pltpu.VMEM((2 * exps, CAP, slot_rows, 128), bf16),
            pltpu.VMEM((block * slot_rows, 128), f32),
            pltpu.VMEM((2, 8 * block, half + 128), bf16),
            pltpu.VMEM((2, hidden_units + inner, half), bf16),
            pltpu.VMEM((2, inner, half), bf16),
            pltpu.VMEM((4 * block, inner), bf16),
            pltpu.VMEM((2, 4 * block, half), bf16),
            pltpu.VMEM((2, 4 * block, half), bf16),
            pltpu.VMEM((2, 4 * block, half), f32),
            pltpu.VMEM((2, 3, block, half), bf16),
            pltpu.VMEM((2, block, half // 2), bf16),
            pltpu.VMEM((2, block, half // 2), bf16),
            pltpu.VMEM((2, block, half), bf16),
            pltpu.VMEM((2, block, half), bf16),
            pltpu.VMEM((block, half), bf16),
            pltpu.VMEM((block, half), bf16),
            pltpu.VMEM((2 * exps, CAP, lanes, 128), bf16),
            pltpu.VMEM((block * lanes, 128), f32),
            pltpu.VMEM((2, exps, CAP, lanes, 128), bf16),
            pltpu.VMEM((2 * exps * CAP * lanes, 128), f32),
            dma((10,)),
            dma((2 * exps,)),
            dma((2 * exps,)),
            dma((9,)),
            dma((9,)),
            dma((8,)),
            dma((8,)),
            dma((4,)),
            dma((4,)),
            dma((12,)),
            dma((12,)),
            dma((2,)),
            dma((2,)),
            dma((2 * exps,)),
            dma((2 * exps,)),
            dma,
        ],
        compiler_params=pltpu.CompilerParams(
            collective_id=1, has_side_effects=True, vmem_limit_bytes=62 * 2**20
        ),
    )(disp, hidden, slot_gates, gate, up, down, adapter_in, adapter_out)


def attention_kernel(
    exps,
    queries,
    key_heads,
    value_heads,
    out_proj,
    residual,
    out,
    pairs,
    weights,
    attended,
    part_send,
    part_recv,
    proj_send,
    proj,
    kv_send,
    kv_recv,
    pass_send,
    pass_recv,
    w_send,
    w_recv,
    att_send,
    att_recv,
    part_send_sem,
    part_recv_sem,
    proj_send_sem,
    proj_recv_sem,
    local_sem,
):
    bf16, f32 = jnp.bfloat16, jnp.float32
    seq_rows = queries.shape[0]
    head_width = key_heads.shape[1]
    heads = queries.shape[1] // head_width
    tokens = seq_rows // exps
    columns = out_proj.shape[1]
    length = 16 * seq_rows

    me, z, x_hi, core = place_on_mesh()
    exp = lax.axis_index("exp")
    chip = z * 2 + x_hi
    sibling = (seq_of(z, x_hi, 1 - core), exp)
    across = (seq_of(z, 1 - x_hi, core), exp)

    def chip_peer(step):
        return lax.rem(chip + step, 8) * 2 + core, exp

    def z_peer(step):
        return seq_of(z + step, x_hi, core), exp

    def exp_peer(step):
        return me, lax.rem(exp + step, exps)

    barrier = pltpu.get_barrier_semaphore()

    def greet_chip(step, carry):
        pl.semaphore_signal(barrier, inc=1, device_id=chip_peer(step), device_id_type=MESH)
        return carry

    def greet_exp(step, carry):
        pl.semaphore_signal(barrier, inc=1, device_id=exp_peer(step), device_id_type=MESH)
        return carry

    lax.fori_loop(1, 8, greet_chip, 0)
    lax.fori_loop(1, exps, greet_exp, 0)
    pl.semaphore_signal(barrier, inc=1, device_id=sibling, device_id_type=MESH)
    pairs[me, :, 0:head_width] = key_heads[...]
    pairs[me, :, head_width : 2 * head_width] = value_heads[...]
    pl.semaphore_wait(barrier, 7 + exps - 1 + 1)

    def remote(source, target, send, recv, device):
        return pltpu.make_async_remote_copy(
            src_ref=source,
            dst_ref=target,
            send_sem=send,
            recv_sem=recv,
            device_id=device,
            device_id_type=MESH,
        )

    def kv_copy(step):
        return remote(
            pairs.at[me], pairs.at[me], kv_send.at[step], kv_recv.at[step], chip_peer(step)
        )

    def kv_pass(step):
        at = lax.rem(chip - step + 8, 8) * 2 + core
        return remote(pairs.at[at], pairs.at[at], pass_send.at[step], pass_recv.at[step], sibling)

    def kv_start(step, carry):
        kv_copy(step).start()
        return carry

    def kv_forward(step, carry):
        kv_copy(step).wait_recv()
        kv_pass(step).start()
        return carry

    lax.fori_loop(1, 8, kv_start, 0)
    kv_pass(0).start()

    mine = x_hi * 2 + core
    other = (1 - x_hi) * 2 + core
    w_pair = remote(out_proj, weights.at[mine], w_send.at[0], w_recv.at[0], sibling)
    w_across = remote(out_proj, weights.at[mine], w_send.at[1], w_recv.at[1], across)
    w_pass = remote(weights.at[other], weights.at[other], w_send.at[2], w_recv.at[2], sibling)
    w_keep = pltpu.make_async_copy(out_proj, weights.at[mine], local_sem)
    w_across.start()
    w_pair.start()
    w_keep.start()

    lax.fori_loop(1, 8, kv_forward, 0)

    def kv_arrive(step, carry):
        kv_pass(step).wait_recv()
        return carry

    lax.fori_loop(0, 8, kv_arrive, 0)

    scaling = head_width ** (-0.5)
    allowed = lax.broadcasted_iota(jnp.int32, (seq_rows, length), 1) <= (
        lax.broadcasted_iota(jnp.int32, (seq_rows, length), 0) + me * seq_rows
    )

    def att_copy(head, step):
        at = attended.at[z, :, pl.ds(pl.multiple_of(head * head_width, 128), head_width)]
        index = (step - 1) * heads + head
        return remote(at, at, att_send.at[index], att_recv.at[index], z_peer(step))

    def one_head(head, carry):
        span = pl.ds(pl.multiple_of(head * head_width, 128), head_width)
        all_keys = pairs[:, :, 0:head_width].reshape(length, head_width)
        scores = contract_last(queries[:, span], all_keys) * scaling
        scores = jnp.where(allowed, scores, -1e30)
        highest = jnp.max(scores, axis=1, keepdims=True)
        probs = jnp.exp(scores - highest)
        totals = jnp.sum(probs, axis=1, keepdims=True)
        all_values = pairs[:, :, head_width : 2 * head_width].reshape(length, head_width)
        summed = dot(probs.astype(bf16), all_values)
        attended[z, :, span] = (summed / totals).astype(bf16)
        for step in range(1, Z):
            att_copy(head, step).start()
        return carry

    lax.fori_loop(0, heads, one_head, 0)

    w_across.wait_recv()
    w_pass.start()
    w_keep.wait()
    w_pair.wait_recv()
    w_pass.wait_recv()

    def att_arrive(head, carry):
        for step in range(1, Z):
            att_copy(head, step).wait_recv()
        return carry

    lax.fori_loop(0, heads, att_arrive, 0)

    def part_copy(chunk, step):
        to = lax.rem(exp + step, exps)
        span = pl.ds(chunk * 2 * columns, 2 * columns)
        index = chunk * exps + step
        return remote(
            part_send.at[to, :, span],
            part_recv.at[exp, :, span],
            part_send_sem.at[index],
            part_recv_sem.at[index],
            exp_peer(step),
        )

    for chunk in range(2):
        for piece in range(2):
            block = chunk * 2 + piece
            rows = attended[...].reshape(Z * seq_rows, heads * head_width)
            value = dot(rows, weights[block]).astype(bf16)
            for z_to in range(Z):
                for exp_to in range(exps):
                    start = z_to * seq_rows + exp_to * tokens
                    part_send[
                        exp_to,
                        z_to * tokens : (z_to + 1) * tokens,
                        block * columns : (block + 1) * columns,
                    ] = value[start : start + tokens]

        def part_start(step, carry, chunk=chunk):
            part_copy(chunk, step).start()
            return carry

        lax.fori_loop(1, exps, part_start, 0)

    for chunk in range(2):

        def part_arrive(step, carry, chunk=chunk):
            part_copy(chunk, step).wait_recv()
            return carry

        lax.fori_loop(1, exps, part_arrive, 0)
        span = slice(chunk * 2 * columns, (chunk + 1) * 2 * columns)
        total = part_send[exp, :, span].astype(f32)

        def add(step, total, span=span):
            return total + part_recv[lax.rem(exp + step, exps), :, span].astype(f32)

        total = lax.fori_loop(1, exps, add, total)
        proj_send[:, :, span] = total.astype(bf16).reshape(Z, tokens, 2 * columns)

    def proj_copy(step):
        return remote(
            proj_send.at[lax.rem(z + step, Z)],
            proj.at[z],
            proj_send_sem.at[step],
            proj_recv_sem.at[step],
            z_peer(step),
        )

    for step in range(1, Z):
        proj_copy(step).start()
    proj[z] = proj_send[z]
    for step in range(1, Z):
        proj_copy(step).wait_recv()
    for place in range(Z):
        span = slice(place * 4 * columns, (place + 1) * 4 * columns)
        out[:, span] = (residual[:, span].astype(f32) + proj[place].astype(f32)).astype(bf16)

    def kv_sent(step, carry):
        kv_copy(step).wait_send()
        kv_pass(step).wait_send()
        return carry

    lax.fori_loop(1, 8, kv_sent, 0)
    kv_pass(0).wait_send()
    w_pair.wait_send()
    w_across.wait_send()
    w_pass.wait_send()

    def att_sent(head, carry):
        for step in range(1, Z):
            att_copy(head, step).wait_send()
        return carry

    lax.fori_loop(0, heads, att_sent, 0)

    def part_sent(step, carry):
        for chunk in range(2):
            part_copy(chunk, step).wait_send()
        return carry

    lax.fori_loop(1, exps, part_sent, 0)
    for step in range(1, Z):
        proj_copy(step).wait_send()


def attention_layer(queries, key_heads, value_heads, out_proj, residual):
    bf16 = jnp.bfloat16
    tokens, width = residual.shape
    seq_rows, columns = queries.shape[0], out_proj.shape[1]
    exps = seq_rows // tokens
    head_width = key_heads.shape[1]
    heads = queries.shape[1] // head_width
    dma = pltpu.SemaphoreType.DMA
    vmem = pl.BlockSpec(memory_space=pltpu.VMEM)
    return pl.pallas_call(
        functools.partial(attention_kernel, exps),
        out_shape=jax.ShapeDtypeStruct((tokens, width), bf16),
        in_specs=[vmem] * 5,
        out_specs=vmem,
        scratch_shapes=[
            pltpu.VMEM((16, seq_rows, 2 * head_width), bf16),
            pltpu.VMEM((4,) + out_proj.shape, bf16),
            pltpu.VMEM((Z, seq_rows, heads * head_width), bf16),
            pltpu.VMEM((exps, Z * tokens, 4 * columns), bf16),
            pltpu.VMEM((exps, Z * tokens, 4 * columns), bf16),
            pltpu.VMEM((Z, tokens, 4 * columns), bf16),
            pltpu.VMEM((Z, tokens, 4 * columns), bf16),
            dma((8,)),
            dma((8,)),
            dma((8,)),
            dma((8,)),
            dma((3,)),
            dma((3,)),
            dma((3 * heads,)),
            dma((3 * heads,)),
            dma((2 * exps,)),
            dma((2 * exps,)),
            dma((Z,)),
            dma((Z,)),
            dma,
        ],
        compiler_params=pltpu.CompilerParams(
            collective_id=2, has_side_effects=True, vmem_limit_bytes=48 * 2**20
        ),
    )(queries, key_heads, value_heads, out_proj, residual)


def on_device(
    residual,
    queries,
    key_heads,
    value_heads,
    out_proj,
    norm_gain,
    gate_weight,
    up_weight,
    down_weight,
    adapter_in,
    adapter_out,
    route_ids,
    route_gates,
    adapter_mix,
):
    group_count = lax.axis_size("exp")
    tok_rows = residual.shape[0]
    hidden_state = attention_layer(queries, key_heads, value_heads, out_proj, residual)
    wide = hidden_state.astype(jnp.float32)
    normed = (
        wide * lax.rsqrt(jnp.mean(wide * wide, axis=1, keepdims=True) + 1e-05) * norm_gain
    ).astype(jnp.bfloat16)
    capacity = max(tok_rows * 5 // 16, 2 * tok_rows // group_count)
    pair_expert = route_ids.reshape(-1)
    expert_ids = jnp.arange(group_count, dtype=jnp.int32)
    onehot = (pair_expert[:, None] == expert_ids[None, :]).astype(jnp.int32)
    ranks = jnp.sum((jnp.cumsum(onehot, axis=0) - 1) * onehot, axis=1)
    target = pair_expert * capacity + ranks
    slot_ids = jnp.arange(group_count * capacity, dtype=jnp.int32)
    pair_hit = target[None, :] == slot_ids[:, None]
    pair_token = jnp.arange(2 * tok_rows, dtype=jnp.int32) // 2
    token_ids = jnp.arange(tok_rows, dtype=jnp.int32)
    pair_of_token = (pair_token[:, None] == token_ids[None, :]).astype(jnp.float32)
    placing = jnp.dot(pair_hit.astype(jnp.float32), pair_of_token).astype(jnp.bfloat16)
    send_rows = (
        jnp.dot(placing, normed, preferred_element_type=jnp.float32)
        .astype(jnp.bfloat16)
        .reshape(group_count, capacity, 2, -1, 128)
        .transpose(2, 0, 1, 3, 4)
    )
    send_mix = jnp.dot(
        placing, adapter_mix.astype(jnp.bfloat16), preferred_element_type=jnp.float32
    ).astype(jnp.bfloat16)
    tail = jnp.pad(
        send_mix.reshape(group_count, capacity, 1, -1),
        ((0, 0), (0, 0), (0, 7), (0, 128 - send_mix.shape[1])),
    )
    disp = jnp.concatenate([send_rows, jnp.broadcast_to(tail, (2,) + tail.shape)], axis=3)
    gate_flat = route_gates.reshape(-1)
    weighted = jnp.where(pair_hit, gate_flat[None, :], 0.0)
    slot_gates = jnp.dot(weighted, pair_of_token, precision=lax.Precision.HIGHEST)
    return expert_layer(
        disp,
        hidden_state,
        slot_gates.T,
        gate_weight[0],
        up_weight[0],
        down_weight[0],
        adapter_in[0],
        adapter_out[0],
    )


def solution(mesh):
    in_specs = (
        P(("seq", "exp"), None),
        P("seq", "exp"),
        P("seq", "exp"),
        P("seq", "exp"),
        P("exp", "seq"),
        P(),
        P("exp", "seq", None),
        P("exp", "seq", None),
        P("exp", "seq", None),
        P("exp", "seq", None),
        P("exp", "seq", None),
        P(("seq", "exp"), None),
        P(("seq", "exp"), None),
        P(("seq", "exp"), None),
    )
    out_specs = P(("seq", "exp"), None)
    return jax.shard_map(
        on_device, mesh=mesh, in_specs=in_specs, out_specs=out_specs, check_vma=False
    )
```

```python
import functools

import jax
import jax.numpy as jnp
from jax import lax
from jax.experimental import pallas as pl
from jax.experimental.pallas import tpu as pltpu
from jax.sharding import PartitionSpec as P

RANK = 16


MESH = pl.DeviceIdType.MESH
CAP = 5
Z = 4
PIECES = 3
SLOT_ROWS = 16


def dot(left, right):
    return jnp.dot(left, right, preferred_element_type=jnp.float32)


def contract_last(left, right):
    return lax.dot_general(
        left, right, (((1,), (1,)), ((), ())), preferred_element_type=jnp.float32
    )


def tile_of(size, most):
    while size % most:
        most -= 128
    return most


def place_on_mesh():
    me = lax.axis_index("seq")
    core = lax.rem(me, 2)
    x_hi = lax.rem(me // 2, 2)
    z = me // 4
    return me, z, x_hi, core


def seq_of(z, x_hi, core):
    return lax.rem(z + Z, Z) * 4 + x_hi * 2 + core


def expert_kernel(
    exps,
    hidden,
    gain,
    ids,
    route_gates,
    mix,
    gate_hbm,
    up_hbm,
    down_hbm,
    in_hbm,
    out_hbm,
    out,
    placed_wide,
    disp,
    arrived,
    wide_slots,
    rows,
    w_first,
    w_second,
    units,
    pair_send,
    pair_recv,
    own,
    z_send,
    half_low,
    half_high,
    full_low,
    full_high,
    x_send,
    x_recv,
    wide_send,
    wide_recv,
    back_wide,
    back,
    returned,
    returned_wide,
    returned_rows,
    weight_sems,
    send_sems,
    recv_sems,
    disp_send,
    disp_recv,
    back_send,
    back_recv,
    local_sems,
):
    bf16, f32 = jnp.bfloat16, jnp.float32
    tokens, width = hidden.shape
    half = width // 2
    lanes = half // 128
    run = lanes // PIECES
    piece = run * 128
    hidden_units = gate_hbm.shape[0]
    adapters = in_hbm.shape[0]
    block = 2 * exps * CAP
    many = 4 * block
    peers = 2 * exps
    slots = exps * CAP
    mix_width = mix.shape[1]

    me, z, x_hi, core = place_on_mesh()
    exp = lax.axis_index("exp")
    sibling = (seq_of(z, x_hi, 1 - core), exp)
    above = (seq_of(z + 1, x_hi, core), exp)
    below = (seq_of(z - 1, x_hi, core), exp)
    across = (seq_of(z, 1 - x_hi, core), exp)
    mine = core * exps + exp

    def peer(step):
        at = lax.rem(mine + step, peers)
        return at, (seq_of(z, x_hi, at // exps), lax.rem(at, exps))

    barrier = pltpu.get_barrier_semaphore()

    def greet(step, carry):
        pl.semaphore_signal(barrier, inc=1, device_id=peer(step)[1], device_id_type=MESH)
        return carry

    lax.fori_loop(1, peers, greet, 0)
    for other in (above, below, across):
        pl.semaphore_signal(barrier, inc=1, device_id=other, device_id_type=MESH)

    loads = []
    for side in range(2):
        columns = pl.ds(side * half, half)
        for source, place, start in (
            (gate_hbm, w_first, 0),
            (up_hbm, w_first, hidden_units),
            (in_hbm, w_first, 2 * hidden_units),
            (down_hbm, w_second, 0),
            (out_hbm, w_second, hidden_units),
        ):
            load = pltpu.make_async_copy(
                source.at[:, columns],
                place.at[side, pl.ds(start, source.shape[0]), :],
                weight_sems.at[len(loads)],
            )
            load.start()
            loads.append(load)

    first_row, second_row = ids[0:1, :], ids[1:2, :]
    down_at = lax.broadcasted_iota(jnp.int32, (tokens, tokens), 0)
    along_at = lax.broadcasted_iota(jnp.int32, (tokens, tokens), 1)

    def upright(row):
        return jnp.sum(jnp.where(down_at == along_at, row, 0), axis=1, keepdims=True)

    first, second = upright(first_row), upright(second_row)

    def count(hits, axis):
        return jnp.sum(jnp.where(hits, 1, 0), axis=axis, keepdims=True)

    first_slot_row = first_row * CAP + count((first == first_row) & (down_at < along_at), 0)
    second_slot_row = (
        second_row * CAP
        + count(first == second_row, 0)
        + count((second == second_row) & (down_at < along_at), 0)
    )
    first_slot = first * CAP + count((first == first_row) & (along_at < down_at), 1)
    second_slot = (
        second * CAP
        + count(second == first_row, 1)
        + count((second == second_row) & (along_at < down_at), 1)
    )
    slot_at = lax.broadcasted_iota(jnp.int32, (slots, tokens), 0)
    placing = jnp.where(
        (slot_at == first_slot_row) | (slot_at == second_slot_row), 1.0, 0.0
    ).astype(bf16)
    slot_along = lax.broadcasted_iota(jnp.int32, (tokens, slots), 1)
    slot_gates = jnp.where(slot_along == first_slot, upright(route_gates[0:1, :]), 0.0) + jnp.where(
        slot_along == second_slot, upright(route_gates[1:2, :]), 0.0
    )
    gate_high = slot_gates.astype(bf16)
    rest = slot_gates - gate_high.astype(f32)
    gate_mid = rest.astype(bf16)
    gate_low = (rest - gate_mid.astype(f32)).astype(bf16)

    wide = hidden[...].astype(f32)
    scale = lax.rsqrt(jnp.mean(wide * wide, axis=1, keepdims=True) + 1e-05)

    def place_columns(side, lane):
        columns = slice(side * half + lane * 128, side * half + (lane + 1) * 128)
        normed = (hidden[:, columns].astype(f32) * scale * gain[:, columns]).astype(bf16)
        return dot(placing, normed)

    placed_wide[...] = jnp.zeros_like(placed_wide)
    mix_rows = dot(placing, mix[...].astype(f32).astype(bf16))
    for side in range(2):
        for lane in range(lanes):
            part, at = (0, lane) if lane < run else (1, lane - run)
            start = (side * 2 + part) * slots * SLOT_ROWS + at
            placed_wide[pl.ds(start, slots, stride=SLOT_ROWS), :] = place_columns(side, lane)
        start = side * 2 * slots * SLOT_ROWS + run
        placed_wide[pl.ds(start, slots, stride=SLOT_ROWS), 0:mix_width] = mix_rows
    disp[...] = placed_wide[...].reshape(disp.shape).astype(bf16)

    pl.semaphore_wait(barrier, peers - 1 + 3)

    def remote(source, target, send, recv, device):
        return pltpu.make_async_remote_copy(
            src_ref=source,
            dst_ref=target,
            send_sem=send,
            recv_sem=recv,
            device_id=device,
            device_id_type=MESH,
        )

    started = []

    def begin(source, target, device):
        index = len(started)
        copy = remote(source, target, send_sems.at[index], recv_sems.at[index], device)
        copy.start()
        started.append(copy)
        return copy

    def dispatch(part, step):
        at, device = peer(step)
        return remote(
            disp.at[at // exps, part, lax.rem(at, exps)],
            arrived.at[part, mine],
            disp_send.at[part, step],
            disp_recv.at[part, step],
            device,
        )

    keeps = []
    for part in range(2):

        def dispatch_start(step, carry, part=part):
            dispatch(part, step).start()
            return carry

        lax.fori_loop(1, peers, dispatch_start, 0)
        keep = pltpu.make_async_copy(
            disp.at[core, part, exp], arrived.at[part, mine], local_sems.at[part]
        )
        keep.start()
        keeps.append(keep)

    edges = [0] + [128 + (index + 1) * piece for index in range(PIECES)]
    middles = [
        edges[index] + (edges[index + 1] - edges[index]) // 256 * 128 for index in range(PIECES)
    ]

    def land(part):
        def dispatch_wait(step, carry):
            dispatch(part, step).wait_recv()
            return carry

        lax.fori_loop(1, peers, dispatch_wait, 0)
        keeps[part].wait()
        wide_slots[part] = arrived[part].astype(f32).reshape(block * SLOT_ROWS, 128)
        chosen = [(run, 0)] + [(lane, lane + 1) for lane in range(run)]
        if part == 1:
            chosen = [(lane, run + 1 + lane) for lane in range(lanes - run)]
        for source, target in chosen:
            rows[core, 0:block, target * 128 : (target + 1) * 128] = wide_slots[
                part, pl.ds(source, block, stride=SLOT_ROWS), :
            ].astype(bf16)

    def cell(place, start, stop):
        return rows.at[core, pl.ds(place * block, block), pl.ds(start, stop - start)]

    def move(source, target, index, device, which=None):
        start, stop = edges[index], edges[index + 1]
        if which == 0:
            stop = middles[index]
        if which == 1:
            start = middles[index]
        return begin(cell(source, start, stop), cell(target, start, stop), device)

    handed = {}

    def hand_over(place, index):
        handed[place, index] = move(place, place, index, sibling)

    low, high, opposite, crossed = {}, {}, {}, {}

    def ring_own(index):
        low[0, index] = move(0, 1, index, above)
        high[0, index] = move(0, 2, index, below)

    def cross_own(index):
        crossed[0, index] = move(0, 4, index, across)
        hand_over(0, index)

    def relay(base, index):
        low[base, index].wait_recv()
        opposite[base, index, 0] = move(base + 1, base + 3, index, above, 0)
        if index == 0:
            crossed[1, 0] = move(1, 5, 0, across)
        hand_over(base + 1, index)
        high[base, index].wait_recv()
        opposite[base, index, 1] = move(base + 2, base + 3, index, below, 1)
        if index == 0:
            crossed[2, 0] = move(2, 6, 0, across)
        hand_over(base + 2, index)

    def close(base, index):
        opposite[base, index, 0].wait_recv()
        opposite[base, index, 1].wait_recv()
        if index == 0:
            crossed[3, 0] = move(3, 7, 0, across)
        hand_over(base + 3, index)

    def spread_crossed(index):
        crossed[0, index].wait_recv()
        low[4, index] = move(4, 5, index, above)
        high[4, index] = move(4, 6, index, below)
        hand_over(4, index)

    def take_crossed(place):
        crossed[place, 0].wait_recv()
        hand_over(place + 4, 0)

    land(0)
    ring_own(0)
    land(1)
    for index in range(1, PIECES):
        cross_own(index)
    cross_own(0)
    relay(0, 0)
    spread_crossed(1)
    spread_crossed(2)
    close(0, 0)
    ring_own(1)
    relay(4, 1)
    ring_own(2)
    relay(4, 2)
    for place in range(4):
        take_crossed(place)
    for index in range(1, PIECES):
        close(4, index)

    for load in loads:
        load.wait()
    unit_tile = tile_of(hidden_units, 256)
    adapter_at = lax.broadcasted_iota(jnp.int32, (mix_width, adapters), 1) // RANK
    spread = (
        lax.broadcasted_iota(jnp.int32, (mix_width, adapters), 0)
        == adapter_at + me * (adapters // RANK)
    ).astype(bf16)

    def first_layer(group, between):
        at = pl.ds(group * many, many)
        data = pl.ds(128, half)

        def project(start, size):
            return contract_last(
                rows[0, at, data], w_first[0, pl.ds(start, size), :]
            ) + contract_last(rows[1, at, data], w_first[1, pl.ds(start, size), :])

        scales = dot(rows[0, at, 0:mix_width], spread) / 8.0
        units[:, hidden_units : hidden_units + adapters] = (
            project(2 * hidden_units, adapters) * scales
        ).astype(bf16)
        for start in range(0, hidden_units, unit_tile):
            gate = project(start, unit_tile)
            between[0]()
            upward = project(hidden_units + start, unit_tile)
            units[:, start : start + unit_tile] = (jax.nn.silu(gate) * upward).astype(bf16)
            between[1]()
            between = between[2:]

    out_tile = tile_of(piece, 512)

    def second_layer(group, side, index, target):
        def tile(step, carry):
            start = pl.multiple_of(index * piece + step * out_tile, 128)
            value = dot(units[...], w_second[side, :, pl.ds(start, out_tile)])
            target[group, :, pl.ds(start, out_tile)] = value.astype(target.dtype)
            return carry

        lax.fori_loop(0, piece // out_tile, tile, 0)

    def columns_of(index, which=None):
        start, stop = index * piece, (index + 1) * piece
        middle = start + piece // 256 * 128
        if which == 0:
            stop = middle
        if which == 1:
            start = middle
        return pl.ds(start, stop - start)

    swaps = {}

    def to_sibling(group, index):
        second_layer(group, 1 - core, index, pair_send)
        at = columns_of(index)
        swaps[group, index] = begin(
            pair_send.at[group, :, at], pair_recv.at[group, :, at], sibling
        )

    def pair_sum(group, place, index, which=None):
        columns = columns_of(index, which)
        inner = columns_of(0, which)
        at = pl.ds(place * block, block)
        total = own[group, at, columns] + pair_recv[group, at, columns].astype(f32)
        if group == 0 and index == 0:
            total = total + wide_recv[at, inner].astype(f32)
        return total

    flows = {}

    def z_flow(group, index, place, which, target, device):
        at = columns_of(index, which)
        return begin(z_send.at[group, place - 1, :, at], target.at[group, :, at], device)

    def reduce_own(group, index):
        second_layer(group, core, index, own)
        swaps[group, index].wait_recv()
        both, left, right = (columns_of(index, which) for which in (None, 0, 1))
        z_send[group, 2, :, both] = pair_sum(group, 3, index).astype(bf16)
        flows["half_low", group, index] = z_flow(group, index, 3, 0, half_low, above)
        flows["half_high", group, index] = z_flow(group, index, 3, 1, half_high, below)
        z_send[group, 1, :, right] = pair_sum(group, 2, index, 1).astype(bf16)
        flows["low_1", group, index] = z_flow(group, index, 2, 1, full_low, above)
        z_send[group, 0, :, left] = pair_sum(group, 1, index, 0).astype(bf16)
        flows["high_0", group, index] = z_flow(group, index, 1, 0, full_high, below)
        own[group, 2 * block : 3 * block, left] = pair_sum(group, 2, index, 0)
        own[group, block : 2 * block, right] = pair_sum(group, 1, index, 1)
        own[group, 0:block, both] = pair_sum(group, 0, index)

    def pass_on(group, index):
        left, right = columns_of(index, 0), columns_of(index, 1)
        flows["half_low", group, index].wait_recv()
        z_send[group, 1, :, left] = (
            own[group, 2 * block : 3 * block, left] + half_low[group, :, left].astype(f32)
        ).astype(bf16)
        flows["low_0", group, index] = z_flow(group, index, 2, 0, full_low, above)
        flows["half_high", group, index].wait_recv()
        z_send[group, 0, :, right] = (
            own[group, block : 2 * block, right] + half_high[group, :, right].astype(f32)
        ).astype(bf16)
        flows["high_1", group, index] = z_flow(group, index, 1, 1, full_high, below)

    def settled(group, index):
        for name in ("low_0", "low_1", "high_0", "high_1"):
            flows[name, group, index].wait_recv()
        both = columns_of(index)
        return (
            own[group, 0:block, both]
            + full_low[group, :, both].astype(f32)
            + full_high[group, :, both].astype(f32)
        )

    def all_here(group):
        for place in range(4):
            for index in range(PIECES):
                handed[group * 4 + place, index].wait_recv()

    def nothing():
        return None

    def cross_wide():
        second_layer(1, core, 0, own)
        swaps[1, 0].wait_recv()
        for place in range(4):
            wide_send[place * block : (place + 1) * block, :] = pair_sum(
                1, place, 0
            ).astype(bf16)
        flows["wide"] = begin(wide_send, wide_recv, across)

    crossing = {}

    def cross_settled(index):
        at = columns_of(index)
        x_send[:, at] = settled(1, index).astype(bf16)
        crossing[index] = begin(x_send.at[:, at], x_recv.at[:, at], across)

    all_here(1)
    first_layer(
        1,
        [lambda: relay(0, 1), nothing, lambda: relay(0, 2), nothing],
    )
    to_sibling(1, 0)
    to_sibling(1, 1)
    cross_wide()
    to_sibling(1, 2)
    close(0, 1)
    reduce_own(1, 1)
    close(0, 2)
    reduce_own(1, 2)
    all_here(0)
    first_layer(
        0,
        [lambda: pass_on(1, 1), nothing, lambda: pass_on(1, 2), nothing],
    )
    to_sibling(0, 1)
    to_sibling(0, 2)
    reduce_own(0, 1)
    to_sibling(0, 0)
    reduce_own(0, 2)
    cross_settled(1)
    flows["wide"].wait_recv()
    reduce_own(0, 0)
    cross_settled(2)
    for index in (1, 2, 0):
        pass_on(0, index)

    def give_back(index, step):
        at, device = peer(step)
        return remote(
            back.at[index, at],
            returned.at[index, core, exp],
            back_send.at[index, step],
            back_recv.at[index, step],
            device,
        )

    keeps_back = {}
    for index in (1, 2, 0):
        own[0, 0:block, columns_of(index)] = settled(0, index)
        if index > 0:
            crossing[index].wait_recv()
        for lane in range(run):
            columns = slice(index * piece + lane * 128, index * piece + (lane + 1) * 128)
            value = own[0, 0:block, columns]
            if index > 0:
                value = value + x_recv[:, columns].astype(f32)
            back_wide[index, pl.ds(lane, block, stride=run), :] = value
        back[index] = back_wide[index].reshape(back.shape[1:]).astype(bf16)

        def give_start(step, carry, index=index):
            give_back(index, step).start()
            return carry

        lax.fori_loop(1, peers, give_start, 0)
        keep = pltpu.make_async_copy(
            back.at[index, mine], returned.at[index, core, exp], local_sems.at[2 + index]
        )
        keep.start()
        keeps_back[index] = keep

    for copy in started:
        copy.wait_send()
    for part in range(2):

        def dispatch_sent(step, carry, part=part):
            dispatch(part, step).wait_send()
            return carry

        lax.fori_loop(1, peers, dispatch_sent, 0)
    stacked = jnp.concatenate(
        [gate_high.astype(f32), gate_mid.astype(f32), gate_low.astype(f32)], axis=0
    ).astype(bf16)
    for index in (1, 2, 0):

        def give_wait(step, carry, index=index):
            give_back(index, step).wait()
            return carry

        lax.fori_loop(1, peers, give_wait, 0)
        keeps_back[index].wait()
        returned_wide[...] = returned[index].astype(f32).reshape(2 * slots * run, 128)
        for side in range(2):
            for lane in range(run):
                returned_rows[side, :, lane * 128 : (lane + 1) * 128] = returned_wide[
                    pl.ds(side * slots * run + lane, slots, stride=run), :
                ].astype(bf16)
            routed = dot(stacked, returned_rows[side])
            routed = routed[0:tokens] + (
                routed[tokens : 2 * tokens] + routed[2 * tokens : 3 * tokens]
            )
            columns = slice(side * half + index * piece, side * half + (index + 1) * piece)
            out[:, columns] = (hidden[:, columns].astype(f32) + routed).astype(bf16)


def expert_layer(
    hidden, gain, ids, route_gates, mix, gate, up, down, adapter_in, adapter_out, exps
):
    bf16, f32 = jnp.bfloat16, jnp.float32
    tokens, width = hidden.shape
    half = width // 2
    lanes = half // 128
    run = lanes // PIECES
    block = 2 * exps * CAP
    slots = exps * CAP
    hidden_units, adapters = gate.shape[0], adapter_in.shape[0]
    inner = hidden_units + adapters
    dma = pltpu.SemaphoreType.DMA
    vmem = pl.BlockSpec(memory_space=pltpu.VMEM)
    anywhere = pl.BlockSpec(memory_space=pl.ANY)
    return pl.pallas_call(
        functools.partial(expert_kernel, exps),
        out_shape=jax.ShapeDtypeStruct((tokens, width), bf16),
        in_specs=[vmem] * 5 + [anywhere] * 5,
        out_specs=vmem,
        scratch_shapes=[
            pltpu.VMEM((2 * 2 * slots * SLOT_ROWS, 128), f32),
            pltpu.VMEM((2, 2, exps, CAP, SLOT_ROWS, 128), bf16),
            pltpu.VMEM((2, 2 * exps, CAP, SLOT_ROWS, 128), bf16),
            pltpu.VMEM((2, block * SLOT_ROWS, 128), f32),
            pltpu.VMEM((2, 8 * block, half + 128), bf16),
            pltpu.VMEM((2, hidden_units + inner, half), bf16),
            pltpu.VMEM((2, inner, half), bf16),
            pltpu.VMEM((4 * block, inner), bf16),
            pltpu.VMEM((2, 4 * block, half), bf16),
            pltpu.VMEM((2, 4 * block, half), bf16),
            pltpu.VMEM((2, 4 * block, half), f32),
            pltpu.VMEM((2, 3, block, half), bf16),
            pltpu.VMEM((2, block, half), bf16),
            pltpu.VMEM((2, block, half), bf16),
            pltpu.VMEM((2, block, half), bf16),
            pltpu.VMEM((2, block, half), bf16),
            pltpu.VMEM((block, half), bf16),
            pltpu.VMEM((block, half), bf16),
            pltpu.VMEM((4 * block, run * 128), bf16),
            pltpu.VMEM((4 * block, run * 128), bf16),
            pltpu.VMEM((PIECES, block * run, 128), f32),
            pltpu.VMEM((PIECES, 2 * exps, CAP, run, 128), bf16),
            pltpu.VMEM((PIECES, 2, exps, CAP, run, 128), bf16),
            pltpu.VMEM((2 * slots * run, 128), f32),
            pltpu.VMEM((2, slots, run * 128), bf16),
            dma((10,)),
            dma((108,)),
            dma((108,)),
            dma((2, 2 * exps)),
            dma((2, 2 * exps)),
            dma((PIECES, 2 * exps)),
            dma((PIECES, 2 * exps)),
            dma((2 + PIECES,)),
        ],
        compiler_params=pltpu.CompilerParams(
            collective_id=1, has_side_effects=True, vmem_limit_bytes=62 * 2**20
        ),
    )(
        hidden,
        gain.reshape(1, width),
        ids.T,
        route_gates.T,
        mix,
        gate,
        up,
        down,
        adapter_in,
        adapter_out,
    )


def attention_kernel(
    exps,
    queries,
    key_heads,
    value_heads,
    out_proj,
    residual,
    out,
    held_queries,
    held_residual,
    pairs,
    weights,
    attended,
    part_send,
    part_recv,
    proj_send,
    proj,
    send_sems,
    recv_sems,
    att_send,
    att_recv,
    part_send_sem,
    part_recv_sem,
    proj_send_sem,
    proj_recv_sem,
    local_sems,
):
    bf16, f32 = jnp.bfloat16, jnp.float32
    seq_rows = queries.shape[0]
    head_width = key_heads.shape[1]
    heads = queries.shape[1] // head_width
    tokens = seq_rows // exps
    columns = out_proj.shape[1]
    length = 16 * seq_rows

    me, z, x_hi, core = place_on_mesh()
    exp = lax.axis_index("exp")
    sibling = (seq_of(z, x_hi, 1 - core), exp)
    across = (seq_of(z, 1 - x_hi, core), exp)
    mine = x_hi * 2 + core
    other = (1 - x_hi) * 2 + core

    def z_peer(step):
        return seq_of(z + step, x_hi, core), exp

    def exp_peer(step):
        return me, lax.rem(exp + step, exps)

    barrier = pltpu.get_barrier_semaphore()

    def greet_exp(step, carry):
        pl.semaphore_signal(barrier, inc=1, device_id=exp_peer(step), device_id_type=MESH)
        return carry

    for device in (across, sibling) + tuple(z_peer(step) for step in range(1, Z)):
        pl.semaphore_signal(barrier, inc=1, device_id=device, device_id_type=MESH)
    lax.fori_loop(1, exps, greet_exp, 0)
    loads = []
    for source, target in (
        (key_heads, pairs.at[me, :, pl.ds(0, head_width)]),
        (value_heads, pairs.at[me, :, pl.ds(head_width, head_width)]),
        (queries, held_queries),
        (out_proj, weights.at[mine]),
        (residual, held_residual),
    ):
        load = pltpu.make_async_copy(source, target, local_sems.at[len(loads)])
        load.start()
        loads.append(load)
    pl.semaphore_wait(barrier, 2 + Z - 1 + exps - 1)

    def remote(source, target, send, recv, device):
        return pltpu.make_async_remote_copy(
            src_ref=source,
            dst_ref=target,
            send_sem=send,
            recv_sem=recv,
            device_id=device,
            device_id_type=MESH,
        )

    started = []

    def begin(source, target, device):
        index = len(started)
        copy = remote(source, target, send_sems.at[index], recv_sems.at[index], device)
        copy.start()
        started.append(copy)
        return copy

    def send_pairs(place, device):
        return begin(pairs.at[place], pairs.at[place], device)

    loads[0].wait()
    loads[1].wait()
    beside = seq_of(z, 1 - x_hi, core)
    crossing = send_pairs(me, across)
    rings = [(step, x_hi, send_pairs(me, z_peer(step))) for step in (1, 3, 2)]
    handed = [send_pairs(me, sibling)]
    crossing.wait_recv()
    rings += [(step, 1 - x_hi, send_pairs(beside, z_peer(step))) for step in (1, 3, 2)]
    handed.append(send_pairs(beside, sibling))

    half_depth = out_proj.shape[0] // 2
    tops = [pl.ds(0, half_depth), pl.ds(half_depth, half_depth)]
    w_across = [begin(out_proj.at[top, :], weights.at[mine, top, :], across) for top in tops]
    w_pair = begin(out_proj, weights.at[mine], sibling)

    for step, side, copy in rings:
        copy.wait_recv()
        handed.append(send_pairs(seq_of(z - step + Z, side, core), sibling))
    for copy in handed:
        copy.wait_recv()
    loads[2].wait()

    scaling = head_width ** (-0.5)
    allowed = lax.broadcasted_iota(jnp.int32, (seq_rows, length), 1) <= (
        lax.broadcasted_iota(jnp.int32, (seq_rows, length), 0) + me * seq_rows
    )

    def att_copy(head, step):
        at = attended.at[z, :, pl.ds(pl.multiple_of(head * head_width, 128), head_width)]
        index = (step - 1) * heads + head
        return remote(at, at, att_send.at[index], att_recv.at[index], z_peer(step))

    def one_head(head, carry):
        span = pl.ds(pl.multiple_of(head * head_width, 128), head_width)
        all_keys = pairs[:, :, 0:head_width].reshape(length, head_width)
        scores = contract_last(held_queries[:, span], all_keys) * scaling
        scores = jnp.where(allowed, scores, -1e30)
        highest = jnp.max(scores, axis=1, keepdims=True)
        probs = jnp.exp(scores - highest)
        totals = jnp.sum(probs, axis=1, keepdims=True)
        all_values = pairs[:, :, head_width : 2 * head_width].reshape(length, head_width)
        summed = dot(probs.astype(bf16), all_values)
        attended[z, :, span] = (summed / totals).astype(bf16)
        for step in range(1, Z):
            att_copy(head, step).start()
        return carry

    lax.fori_loop(0, heads, one_head, 0)

    def att_arrive(head, carry):
        for step in range(1, Z):
            att_copy(head, step).wait_recv()
        return carry

    lax.fori_loop(0, heads, att_arrive, 0)

    def part_copy(chunk, first, step):
        to = lax.rem(exp + step, exps)
        span = halves(chunk)
        index = first * exps + step
        return remote(
            part_send.at[to, :, span],
            part_recv.at[exp, :, span],
            part_send_sem.at[index],
            part_recv_sem.at[index],
            exp_peer(step),
        )

    def halves(chunk):
        return pl.ds(pl.multiple_of(chunk * 2 * columns, 128), 2 * columns)

    def project(chunk, first):
        for piece in range(2):
            block = chunk * 2 + piece
            at = pl.ds(pl.multiple_of(block * columns, 128), columns)
            rows = attended[...].reshape(Z * seq_rows, heads * head_width)
            value = dot(rows, weights[block]).astype(bf16)
            for z_to in range(Z):
                for exp_to in range(exps):
                    start = z_to * seq_rows + exp_to * tokens
                    part_send[exp_to, z_to * tokens : (z_to + 1) * tokens, at] = value[
                        start : start + tokens
                    ]

        def part_start(step, carry):
            part_copy(chunk, first, step).start()
            return carry

        lax.fori_loop(1, exps, part_start, 0)

    def total_of(chunk, first):
        def part_arrive(step, carry):
            part_copy(chunk, first, step).wait_recv()
            return carry

        lax.fori_loop(1, exps, part_arrive, 0)
        span = halves(chunk)

        def add(step, total):
            return total + part_recv[lax.rem(exp + step, exps), :, span].astype(f32)

        total = lax.fori_loop(1, exps, add, part_send[exp, :, span].astype(f32))
        proj_send[:, :, span] = total.astype(bf16).reshape(Z, tokens, 2 * columns)

    loads[3].wait()
    w_pair.wait_recv()
    project(x_hi, 0)
    w_pass = []
    for index, top in enumerate(tops):
        w_across[index].wait_recv()
        at = weights.at[other, top, :]
        w_pass.append(begin(at, at, sibling))
    for copy in w_pass:
        copy.wait_recv()
    project(1 - x_hi, 1)
    total_of(x_hi, 0)
    total_of(1 - x_hi, 1)
    loads[4].wait()

    def proj_copy(step):
        return remote(
            proj_send.at[lax.rem(z + step, Z)],
            proj.at[z],
            proj_send_sem.at[step],
            proj_recv_sem.at[step],
            z_peer(step),
        )

    for step in range(1, Z):
        proj_copy(step).start()
    proj[z] = proj_send[z]
    for step in range(1, Z):
        proj_copy(step).wait_recv()
    for place in range(Z):
        span = slice(place * 4 * columns, (place + 1) * 4 * columns)
        out[:, span] = (held_residual[:, span].astype(f32) + proj[place].astype(f32)).astype(bf16)

    for copy in started:
        copy.wait_send()

    def att_sent(head, carry):
        for step in range(1, Z):
            att_copy(head, step).wait_send()
        return carry

    lax.fori_loop(0, heads, att_sent, 0)

    def part_sent(step, carry):
        part_copy(x_hi, 0, step).wait_send()
        part_copy(1 - x_hi, 1, step).wait_send()
        return carry

    lax.fori_loop(1, exps, part_sent, 0)
    for step in range(1, Z):
        proj_copy(step).wait_send()


def attention_layer(queries, key_heads, value_heads, out_proj, residual):
    bf16 = jnp.bfloat16
    tokens, width = residual.shape
    seq_rows, columns = queries.shape[0], out_proj.shape[1]
    exps = seq_rows // tokens
    head_width = key_heads.shape[1]
    heads = queries.shape[1] // head_width
    dma = pltpu.SemaphoreType.DMA
    vmem = pl.BlockSpec(memory_space=pltpu.VMEM)
    return pl.pallas_call(
        functools.partial(attention_kernel, exps),
        out_shape=jax.ShapeDtypeStruct((tokens, width), bf16),
        in_specs=[pl.BlockSpec(memory_space=pl.ANY)] * 5,
        out_specs=vmem,
        scratch_shapes=[
            pltpu.VMEM(queries.shape, bf16),
            pltpu.VMEM(residual.shape, bf16),
            pltpu.VMEM((16, seq_rows, 2 * head_width), bf16),
            pltpu.VMEM((4,) + out_proj.shape, bf16),
            pltpu.VMEM((Z, seq_rows, heads * head_width), bf16),
            pltpu.VMEM((exps, Z * tokens, 4 * columns), bf16),
            pltpu.VMEM((exps, Z * tokens, 4 * columns), bf16),
            pltpu.VMEM((Z, tokens, 4 * columns), bf16),
            pltpu.VMEM((Z, tokens, 4 * columns), bf16),
            dma((20,)),
            dma((20,)),
            dma((3 * heads,)),
            dma((3 * heads,)),
            dma((2 * exps,)),
            dma((2 * exps,)),
            dma((Z,)),
            dma((Z,)),
            dma((5,)),
        ],
        compiler_params=pltpu.CompilerParams(
            collective_id=2, has_side_effects=True, vmem_limit_bytes=62 * 2**20
        ),
    )(queries, key_heads, value_heads, out_proj, residual)


def on_device(
    residual,
    queries,
    key_heads,
    value_heads,
    out_proj,
    norm_gain,
    gate_weight,
    up_weight,
    down_weight,
    adapter_in,
    adapter_out,
    route_ids,
    route_gates,
    adapter_mix,
):
    hidden_state = attention_layer(queries, key_heads, value_heads, out_proj, residual)
    return expert_layer(
        hidden_state,
        norm_gain,
        route_ids,
        route_gates,
        adapter_mix,
        gate_weight[0],
        up_weight[0],
        down_weight[0],
        adapter_in[0],
        adapter_out[0],
        lax.axis_size("exp"),
    )


def solution(mesh):
    in_specs = (
        P(("seq", "exp"), None),
        P("seq", "exp"),
        P("seq", "exp"),
        P("seq", "exp"),
        P("exp", "seq"),
        P(),
        P("exp", "seq", None),
        P("exp", "seq", None),
        P("exp", "seq", None),
        P("exp", "seq", None),
        P("exp", "seq", None),
        P(("seq", "exp"), None),
        P(("seq", "exp"), None),
        P(("seq", "exp"), None),
    )
    out_specs = P(("seq", "exp"), None)
    return jax.shard_map(
        on_device, mesh=mesh, in_specs=in_specs, out_specs=out_specs, check_vma=False
    )
```

```python
import functools

import jax
import jax.numpy as jnp
from jax import lax
from jax.experimental import pallas as pl
from jax.experimental.pallas import tpu as pltpu
from jax.sharding import PartitionSpec as P

RANK = 16


MESH = pl.DeviceIdType.MESH
CAP = 5
Z = 4
PIECES = 3
SLOT_ROWS = 16


def dot(left, right):
    return jnp.dot(left, right, preferred_element_type=jnp.float32)


def contract_last(left, right):
    return lax.dot_general(
        left, right, (((1,), (1,)), ((), ())), preferred_element_type=jnp.float32
    )


def tile_of(size, most):
    while size % most:
        most -= 128
    return most


def place_on_mesh():
    me = lax.axis_index("seq")
    core = lax.rem(me, 2)
    x_hi = lax.rem(me // 2, 2)
    z = me // 4
    return me, z, x_hi, core


def seq_of(z, x_hi, core):
    return lax.rem(z + Z, Z) * 4 + x_hi * 2 + core


def expert_kernel(
    exps,
    hidden,
    gain,
    ids,
    route_gates,
    mix,
    gate_hbm,
    up_hbm,
    down_hbm,
    in_hbm,
    out_hbm,
    out,
    placed_wide,
    disp,
    arrived,
    wide_slots,
    rows,
    w_first,
    w_second,
    units,
    pair_send,
    pair_recv,
    own,
    z_send,
    half_low,
    half_high,
    full_low,
    full_high,
    x_send,
    x_recv,
    wide_send,
    wide_recv,
    back_wide,
    back,
    returned,
    returned_wide,
    returned_rows,
    weight_sems,
    send_sems,
    recv_sems,
    disp_send,
    disp_recv,
    back_send,
    back_recv,
    local_sems,
):
    bf16, f32 = jnp.bfloat16, jnp.float32
    tokens, width = hidden.shape
    half = width // 2
    lanes = half // 128
    run = lanes // PIECES
    piece = run * 128
    hidden_units = gate_hbm.shape[0]
    adapters = in_hbm.shape[0]
    block = 2 * exps * CAP
    many = 4 * block
    peers = 2 * exps
    slots = exps * CAP
    mix_width = mix.shape[1]

    me, z, x_hi, core = place_on_mesh()
    exp = lax.axis_index("exp")
    sibling = (seq_of(z, x_hi, 1 - core), exp)
    above = (seq_of(z + 1, x_hi, core), exp)
    below = (seq_of(z - 1, x_hi, core), exp)
    across = (seq_of(z, 1 - x_hi, core), exp)
    mine = core * exps + exp

    def peer(step):
        at = lax.rem(mine + step, peers)
        return at, (seq_of(z, x_hi, at // exps), lax.rem(at, exps))

    barrier = pltpu.get_barrier_semaphore()

    def greet(step, carry):
        pl.semaphore_signal(barrier, inc=1, device_id=peer(step)[1], device_id_type=MESH)
        return carry

    lax.fori_loop(1, peers, greet, 0)
    for other in (above, below, across):
        pl.semaphore_signal(barrier, inc=1, device_id=other, device_id_type=MESH)

    loads = []
    for side in range(2):
        columns = pl.ds(side * half, half)
        for source, place, start in (
            (gate_hbm, w_first, 0),
            (up_hbm, w_first, hidden_units),
            (in_hbm, w_first, 2 * hidden_units),
            (down_hbm, w_second, 0),
            (out_hbm, w_second, hidden_units),
        ):
            load = pltpu.make_async_copy(
                source.at[:, columns],
                place.at[side, pl.ds(start, source.shape[0]), :],
                weight_sems.at[len(loads)],
            )
            load.start()
            loads.append(load)

    first_row, second_row = ids[0:1, :], ids[1:2, :]
    down_at = lax.broadcasted_iota(jnp.int32, (tokens, tokens), 0)
    along_at = lax.broadcasted_iota(jnp.int32, (tokens, tokens), 1)

    def upright(row):
        return jnp.sum(jnp.where(down_at == along_at, row, 0), axis=1, keepdims=True)

    first, second = upright(first_row), upright(second_row)

    def count(hits, axis):
        return jnp.sum(jnp.where(hits, 1, 0), axis=axis, keepdims=True)

    first_slot_row = first_row * CAP + count((first == first_row) & (down_at < along_at), 0)
    second_slot_row = (
        second_row * CAP
        + count(first == second_row, 0)
        + count((second == second_row) & (down_at < along_at), 0)
    )
    first_slot = first * CAP + count((first == first_row) & (along_at < down_at), 1)
    second_slot = (
        second * CAP
        + count(second == first_row, 1)
        + count((second == second_row) & (along_at < down_at), 1)
    )
    slot_at = lax.broadcasted_iota(jnp.int32, (slots, tokens), 0)
    placing = jnp.where(
        (slot_at == first_slot_row) | (slot_at == second_slot_row), 1.0, 0.0
    ).astype(bf16)
    slot_along = lax.broadcasted_iota(jnp.int32, (tokens, slots), 1)
    slot_gates = jnp.where(slot_along == first_slot, upright(route_gates[0:1, :]), 0.0) + jnp.where(
        slot_along == second_slot, upright(route_gates[1:2, :]), 0.0
    )
    gate_high = slot_gates.astype(bf16)
    rest = slot_gates - gate_high.astype(f32)
    gate_mid = rest.astype(bf16)
    gate_low = (rest - gate_mid.astype(f32)).astype(bf16)

    wide = hidden[...].astype(f32)
    scale = lax.rsqrt(jnp.mean(wide * wide, axis=1, keepdims=True) + 1e-05)

    def place_columns(side, lane):
        columns = slice(side * half + lane * 128, side * half + (lane + 1) * 128)
        normed = (hidden[:, columns].astype(f32) * scale * gain[:, columns]).astype(bf16)
        return dot(placing, normed)

    placed_wide[...] = jnp.zeros_like(placed_wide)
    mix_rows = dot(placing, mix[...].astype(f32).astype(bf16))
    for side in range(2):
        for lane in range(lanes):
            part, at = (0, lane) if lane < run else (1, lane - run)
            start = (side * 2 + part) * slots * SLOT_ROWS + at
            placed_wide[pl.ds(start, slots, stride=SLOT_ROWS), :] = place_columns(side, lane)
        start = side * 2 * slots * SLOT_ROWS + run
        placed_wide[pl.ds(start, slots, stride=SLOT_ROWS), 0:mix_width] = mix_rows
    disp[...] = placed_wide[...].reshape(disp.shape).astype(bf16)

    pl.semaphore_wait(barrier, peers - 1 + 3)

    def remote(source, target, send, recv, device):
        return pltpu.make_async_remote_copy(
            src_ref=source,
            dst_ref=target,
            send_sem=send,
            recv_sem=recv,
            device_id=device,
            device_id_type=MESH,
        )

    started = []

    def begin(source, target, device):
        index = len(started)
        copy = remote(source, target, send_sems.at[index], recv_sems.at[index], device)
        copy.start()
        started.append(copy)
        return copy

    def dispatch(part, step):
        at, device = peer(step)
        return remote(
            disp.at[at // exps, part, lax.rem(at, exps)],
            arrived.at[part, mine],
            disp_send.at[part, step],
            disp_recv.at[part, step],
            device,
        )

    keeps = []
    for part in range(2):

        def dispatch_start(step, carry, part=part):
            dispatch(part, step).start()
            return carry

        lax.fori_loop(1, peers, dispatch_start, 0)
        keep = pltpu.make_async_copy(
            disp.at[core, part, exp], arrived.at[part, mine], local_sems.at[part]
        )
        keep.start()
        keeps.append(keep)

    edges = [0] + [128 + (index + 1) * piece for index in range(PIECES)]
    middles = [
        edges[index] + (edges[index + 1] - edges[index]) // 256 * 128 for index in range(PIECES)
    ]

    def land(part):
        def dispatch_wait(step, carry):
            dispatch(part, step).wait_recv()
            return carry

        lax.fori_loop(1, peers, dispatch_wait, 0)
        keeps[part].wait()
        wide_slots[part] = arrived[part].astype(f32).reshape(block * SLOT_ROWS, 128)
        chosen = [(run, 0)] + [(lane, lane + 1) for lane in range(run)]
        if part == 1:
            chosen = [(lane, run + 1 + lane) for lane in range(lanes - run)]
        for source, target in chosen:
            rows[core, 0:block, target * 128 : (target + 1) * 128] = wide_slots[
                part, pl.ds(source, block, stride=SLOT_ROWS), :
            ].astype(bf16)

    def cell(place, start, stop):
        return rows.at[core, pl.ds(place * block, block), pl.ds(start, stop - start)]

    def move(source, target, index, device, which=None):
        start, stop = edges[index], edges[index + 1]
        if which == 0:
            stop = middles[index]
        if which == 1:
            start = middles[index]
        return begin(cell(source, start, stop), cell(target, start, stop), device)

    handed = {}

    def hand_over(place, index):
        handed[place, index] = move(place, place, index, sibling)

    low, high, opposite, crossed = {}, {}, {}, {}

    def ring_own(index):
        low[0, index] = move(0, 1, index, above)
        high[0, index] = move(0, 2, index, below)

    def cross_own(index):
        crossed[0, index] = move(0, 4, index, across)
        hand_over(0, index)

    def relay(base, index):
        low[base, index].wait_recv()
        opposite[base, index, 0] = move(base + 1, base + 3, index, above, 0)
        if index == 0:
            crossed[1, 0] = move(1, 5, 0, across)
        hand_over(base + 1, index)
        high[base, index].wait_recv()
        opposite[base, index, 1] = move(base + 2, base + 3, index, below, 1)
        if index == 0:
            crossed[2, 0] = move(2, 6, 0, across)
        hand_over(base + 2, index)

    def close(base, index):
        opposite[base, index, 0].wait_recv()
        opposite[base, index, 1].wait_recv()
        if index == 0:
            crossed[3, 0] = move(3, 7, 0, across)
        hand_over(base + 3, index)

    def spread_crossed(index):
        crossed[0, index].wait_recv()
        low[4, index] = move(4, 5, index, above)
        high[4, index] = move(4, 6, index, below)
        hand_over(4, index)

    def take_crossed(place):
        crossed[place, 0].wait_recv()
        hand_over(place + 4, 0)

    land(0)
    ring_own(0)
    land(1)
    for index in range(1, PIECES):
        cross_own(index)
    ring_own(1)
    cross_own(0)
    relay(0, 0)
    spread_crossed(1)
    spread_crossed(2)
    ring_own(2)
    close(0, 0)
    relay(4, 1)
    relay(4, 2)
    for place in range(4):
        take_crossed(place)
    for index in range(1, PIECES):
        close(4, index)

    for load in loads:
        load.wait()
    unit_tile = tile_of(hidden_units, 256)
    adapter_at = lax.broadcasted_iota(jnp.int32, (mix_width, adapters), 1) // RANK
    spread = (
        lax.broadcasted_iota(jnp.int32, (mix_width, adapters), 0)
        == adapter_at + me * (adapters // RANK)
    ).astype(bf16)

    def first_layer(group, between):
        at = pl.ds(group * many, many)
        data = pl.ds(128, half)

        def project(start, size):
            return contract_last(
                rows[0, at, data], w_first[0, pl.ds(start, size), :]
            ) + contract_last(rows[1, at, data], w_first[1, pl.ds(start, size), :])

        scales = dot(rows[0, at, 0:mix_width], spread) / 8.0
        units[:, hidden_units : hidden_units + adapters] = (
            project(2 * hidden_units, adapters) * scales
        ).astype(bf16)
        for start in range(0, hidden_units, unit_tile):
            gate = project(start, unit_tile)
            between[0]()
            upward = project(hidden_units + start, unit_tile)
            units[:, start : start + unit_tile] = (jax.nn.silu(gate) * upward).astype(bf16)
            between[1]()
            between = between[2:]

    out_tile = tile_of(piece, 1024)

    def second_layer(group, side, index, target):
        def tile(step, carry):
            start = pl.multiple_of(index * piece + step * out_tile, 128)
            value = dot(units[...], w_second[side, :, pl.ds(start, out_tile)])
            target[group, :, pl.ds(start, out_tile)] = value.astype(target.dtype)
            return carry

        lax.fori_loop(0, piece // out_tile, tile, 0)

    def columns_of(index, which=None):
        start, stop = index * piece, (index + 1) * piece
        middle = start + piece // 256 * 128
        if which == 0:
            stop = middle
        if which == 1:
            start = middle
        return pl.ds(start, stop - start)

    swaps = {}

    def to_sibling(group, index):
        second_layer(group, 1 - core, index, pair_send)
        at = columns_of(index)
        swaps[group, index] = begin(
            pair_send.at[group, :, at], pair_recv.at[group, :, at], sibling
        )

    def pair_sum(group, place, index, which=None):
        columns = columns_of(index, which)
        inner = columns_of(0, which)
        at = pl.ds(place * block, block)
        total = own[group, at, columns] + pair_recv[group, at, columns].astype(f32)
        if group == 0 and index == 0:
            total = total + wide_recv[at, inner].astype(f32)
        return total

    flows = {}

    def z_flow(group, index, place, which, target, device):
        at = columns_of(index, which)
        return begin(z_send.at[group, place - 1, :, at], target.at[group, :, at], device)

    def reduce_own(group, index):
        second_layer(group, core, index, own)
        swaps[group, index].wait_recv()
        both, left, right = (columns_of(index, which) for which in (None, 0, 1))
        z_send[group, 2, :, both] = pair_sum(group, 3, index).astype(bf16)
        flows["half_low", group, index] = z_flow(group, index, 3, 0, half_low, above)
        flows["half_high", group, index] = z_flow(group, index, 3, 1, half_high, below)
        z_send[group, 1, :, right] = pair_sum(group, 2, index, 1).astype(bf16)
        flows["low_1", group, index] = z_flow(group, index, 2, 1, full_low, above)
        z_send[group, 0, :, left] = pair_sum(group, 1, index, 0).astype(bf16)
        flows["high_0", group, index] = z_flow(group, index, 1, 0, full_high, below)
        own[group, 2 * block : 3 * block, left] = pair_sum(group, 2, index, 0)
        own[group, block : 2 * block, right] = pair_sum(group, 1, index, 1)
        own[group, 0:block, both] = pair_sum(group, 0, index)

    def pass_on(group, index):
        left, right = columns_of(index, 0), columns_of(index, 1)
        flows["half_low", group, index].wait_recv()
        z_send[group, 1, :, left] = (
            own[group, 2 * block : 3 * block, left] + half_low[group, :, left].astype(f32)
        ).astype(bf16)
        flows["low_0", group, index] = z_flow(group, index, 2, 0, full_low, above)
        flows["half_high", group, index].wait_recv()
        z_send[group, 0, :, right] = (
            own[group, block : 2 * block, right] + half_high[group, :, right].astype(f32)
        ).astype(bf16)
        flows["high_1", group, index] = z_flow(group, index, 1, 1, full_high, below)

    def settled(group, index):
        for name in ("low_0", "low_1", "high_0", "high_1"):
            flows[name, group, index].wait_recv()
        both = columns_of(index)
        return (
            own[group, 0:block, both]
            + full_low[group, :, both].astype(f32)
            + full_high[group, :, both].astype(f32)
        )

    def all_here(group):
        for place in range(4):
            for index in range(PIECES):
                handed[group * 4 + place, index].wait_recv()

    def nothing():
        return None

    def cross_wide():
        second_layer(1, core, 0, own)
        swaps[1, 0].wait_recv()
        for place in range(4):
            wide_send[place * block : (place + 1) * block, :] = pair_sum(
                1, place, 0
            ).astype(bf16)
        flows["wide"] = begin(wide_send, wide_recv, across)

    crossing = {}

    def cross_settled(index):
        at = columns_of(index)
        x_send[:, at] = settled(1, index).astype(bf16)
        crossing[index] = begin(x_send.at[:, at], x_recv.at[:, at], across)

    all_here(1)
    first_layer(
        1,
        [lambda: relay(0, 1), nothing, lambda: relay(0, 2), nothing],
    )
    to_sibling(1, 0)
    to_sibling(1, 1)
    cross_wide()
    to_sibling(1, 2)
    close(0, 1)
    reduce_own(1, 1)
    close(0, 2)
    reduce_own(1, 2)
    all_here(0)
    first_layer(
        0,
        [lambda: pass_on(1, 1), nothing, lambda: pass_on(1, 2), nothing],
    )
    to_sibling(0, 1)
    to_sibling(0, 2)
    reduce_own(0, 1)
    to_sibling(0, 0)
    reduce_own(0, 2)
    cross_settled(1)
    flows["wide"].wait_recv()
    reduce_own(0, 0)
    cross_settled(2)
    for index in (1, 2, 0):
        pass_on(0, index)

    def give_back(index, step):
        at, device = peer(step)
        return remote(
            back.at[index, at],
            returned.at[index, core, exp],
            back_send.at[index, step],
            back_recv.at[index, step],
            device,
        )

    keeps_back = {}
    for index in (1, 2, 0):
        own[0, 0:block, columns_of(index)] = settled(0, index)
        if index > 0:
            crossing[index].wait_recv()
        for lane in range(run):
            columns = slice(index * piece + lane * 128, index * piece + (lane + 1) * 128)
            value = own[0, 0:block, columns]
            if index > 0:
                value = value + x_recv[:, columns].astype(f32)
            back_wide[index, pl.ds(lane, block, stride=run), :] = value
        back[index] = back_wide[index].reshape(back.shape[1:]).astype(bf16)

        def give_start(step, carry, index=index):
            give_back(index, step).start()
            return carry

        lax.fori_loop(1, peers, give_start, 0)
        keep = pltpu.make_async_copy(
            back.at[index, mine], returned.at[index, core, exp], local_sems.at[2 + index]
        )
        keep.start()
        keeps_back[index] = keep

    for copy in started:
        copy.wait_send()
    for part in range(2):

        def dispatch_sent(step, carry, part=part):
            dispatch(part, step).wait_send()
            return carry

        lax.fori_loop(1, peers, dispatch_sent, 0)
    stacked = jnp.concatenate(
        [gate_high.astype(f32), gate_mid.astype(f32), gate_low.astype(f32)], axis=0
    ).astype(bf16)
    for index in (1, 2, 0):

        def give_wait(step, carry, index=index):
            give_back(index, step).wait()
            return carry

        lax.fori_loop(1, peers, give_wait, 0)
        keeps_back[index].wait()
        returned_wide[...] = returned[index].astype(f32).reshape(2 * slots * run, 128)
        for side in range(2):
            for lane in range(run):
                returned_rows[side, :, lane * 128 : (lane + 1) * 128] = returned_wide[
                    pl.ds(side * slots * run + lane, slots, stride=run), :
                ].astype(bf16)
            routed = dot(stacked, returned_rows[side])
            routed = routed[0:tokens] + (
                routed[tokens : 2 * tokens] + routed[2 * tokens : 3 * tokens]
            )
            columns = slice(side * half + index * piece, side * half + (index + 1) * piece)
            out[:, columns] = (hidden[:, columns].astype(f32) + routed).astype(bf16)


def expert_layer(
    hidden, gain, ids, route_gates, mix, gate, up, down, adapter_in, adapter_out, exps
):
    bf16, f32 = jnp.bfloat16, jnp.float32
    tokens, width = hidden.shape
    half = width // 2
    lanes = half // 128
    run = lanes // PIECES
    block = 2 * exps * CAP
    slots = exps * CAP
    hidden_units, adapters = gate.shape[0], adapter_in.shape[0]
    inner = hidden_units + adapters
    dma = pltpu.SemaphoreType.DMA
    vmem = pl.BlockSpec(memory_space=pltpu.VMEM)
    anywhere = pl.BlockSpec(memory_space=pl.ANY)
    return pl.pallas_call(
        functools.partial(expert_kernel, exps),
        out_shape=jax.ShapeDtypeStruct((tokens, width), bf16),
        in_specs=[vmem] * 5 + [anywhere] * 5,
        out_specs=vmem,
        scratch_shapes=[
            pltpu.VMEM((2 * 2 * slots * SLOT_ROWS, 128), f32),
            pltpu.VMEM((2, 2, exps, CAP, SLOT_ROWS, 128), bf16),
            pltpu.VMEM((2, 2 * exps, CAP, SLOT_ROWS, 128), bf16),
            pltpu.VMEM((2, block * SLOT_ROWS, 128), f32),
            pltpu.VMEM((2, 8 * block, half + 128), bf16),
            pltpu.VMEM((2, hidden_units + inner, half), bf16),
            pltpu.VMEM((2, inner, half), bf16),
            pltpu.VMEM((4 * block, inner), bf16),
            pltpu.VMEM((2, 4 * block, half), bf16),
            pltpu.VMEM((2, 4 * block, half), bf16),
            pltpu.VMEM((2, 4 * block, half), f32),
            pltpu.VMEM((2, 3, block, half), bf16),
            pltpu.VMEM((2, block, half), bf16),
            pltpu.VMEM((2, block, half), bf16),
            pltpu.VMEM((2, block, half), bf16),
            pltpu.VMEM((2, block, half), bf16),
            pltpu.VMEM((block, half), bf16),
            pltpu.VMEM((block, half), bf16),
            pltpu.VMEM((4 * block, run * 128), bf16),
            pltpu.VMEM((4 * block, run * 128), bf16),
            pltpu.VMEM((PIECES, block * run, 128), f32),
            pltpu.VMEM((PIECES, 2 * exps, CAP, run, 128), bf16),
            pltpu.VMEM((PIECES, 2, exps, CAP, run, 128), bf16),
            pltpu.VMEM((2 * slots * run, 128), f32),
            pltpu.VMEM((2, slots, run * 128), bf16),
            dma((10,)),
            dma((108,)),
            dma((108,)),
            dma((2, 2 * exps)),
            dma((2, 2 * exps)),
            dma((PIECES, 2 * exps)),
            dma((PIECES, 2 * exps)),
            dma((2 + PIECES,)),
        ],
        compiler_params=pltpu.CompilerParams(
            collective_id=1, has_side_effects=True, vmem_limit_bytes=62 * 2**20
        ),
    )(
        hidden,
        gain.reshape(1, width),
        ids.T,
        route_gates.T,
        mix,
        gate,
        up,
        down,
        adapter_in,
        adapter_out,
    )


def attention_kernel(
    exps,
    queries,
    key_heads,
    value_heads,
    out_proj,
    residual,
    out,
    held_queries,
    held_residual,
    pairs,
    weights,
    attended,
    part_send,
    part_recv,
    proj_send,
    proj,
    kv_send,
    kv_recv,
    pass_send,
    pass_recv,
    send_sems,
    recv_sems,
    att_send,
    att_recv,
    part_send_sem,
    part_recv_sem,
    proj_send_sem,
    proj_recv_sem,
    local_sems,
):
    bf16, f32 = jnp.bfloat16, jnp.float32
    seq_rows = queries.shape[0]
    head_width = key_heads.shape[1]
    heads = queries.shape[1] // head_width
    tokens = seq_rows // exps
    columns = out_proj.shape[1]
    length = 16 * seq_rows

    me, z, x_hi, core = place_on_mesh()
    exp = lax.axis_index("exp")
    sibling = (seq_of(z, x_hi, 1 - core), exp)
    across = (seq_of(z, 1 - x_hi, core), exp)
    chip = z * 2 + x_hi
    mine = x_hi * 2 + core
    other = (1 - x_hi) * 2 + core

    def z_peer(step):
        return seq_of(z + step, x_hi, core), exp

    def exp_peer(step):
        return me, lax.rem(exp + step, exps)

    barrier = pltpu.get_barrier_semaphore()

    def greet_exp(step, carry):
        pl.semaphore_signal(barrier, inc=1, device_id=exp_peer(step), device_id_type=MESH)
        return carry

    def chip_peer(step):
        return lax.rem(chip + step, 8) * 2 + core, exp

    def greet_chip(step, carry):
        pl.semaphore_signal(barrier, inc=1, device_id=chip_peer(step), device_id_type=MESH)
        return carry

    pairs[...] = jnp.zeros_like(pairs)
    pl.semaphore_signal(barrier, inc=1, device_id=sibling, device_id_type=MESH)
    lax.fori_loop(1, 8, greet_chip, 0)
    lax.fori_loop(1, exps, greet_exp, 0)
    loads = []
    for source, target in (
        (key_heads, pairs.at[me, :, pl.ds(0, head_width)]),
        (value_heads, pairs.at[me, :, pl.ds(head_width, head_width)]),
        (queries, held_queries),
        (out_proj, weights.at[mine]),
        (residual, held_residual),
    ):
        load = pltpu.make_async_copy(source, target, local_sems.at[len(loads)])
        load.start()
        loads.append(load)
    pl.semaphore_wait(barrier, 1 + 7 + exps - 1)

    def remote(source, target, send, recv, device):
        return pltpu.make_async_remote_copy(
            src_ref=source,
            dst_ref=target,
            send_sem=send,
            recv_sem=recv,
            device_id=device,
            device_id_type=MESH,
        )

    started = []

    def begin(source, target, device):
        index = len(started)
        copy = remote(source, target, send_sems.at[index], recv_sems.at[index], device)
        copy.start()
        started.append(copy)
        return copy

    def kv_copy(step):
        return remote(
            pairs.at[me], pairs.at[me], kv_send.at[step], kv_recv.at[step], chip_peer(step)
        )

    def kv_pass(step):
        at = lax.rem(chip - step + 8, 8) * 2 + core
        return remote(pairs.at[at], pairs.at[at], pass_send.at[step], pass_recv.at[step], sibling)

    def kv_start(step, carry):
        @pl.when(chip + step < 8)
        def _():
            kv_copy(step).start()

        return carry

    def kv_forward(step, carry):
        @pl.when(chip - step >= 0)
        def _():
            kv_copy(step).wait_recv()
            kv_pass(step).start()

        return carry

    def kv_arrive(step, carry):
        @pl.when(chip - step >= 0)
        def _():
            kv_pass(step).wait_recv()

        return carry

    def kv_sent(step, carry):
        @pl.when(chip + step < 8)
        def _():
            kv_copy(step).wait_send()

        @pl.when(chip - step >= 0)
        def _():
            kv_pass(step).wait_send()

        return carry

    loads[0].wait()
    loads[1].wait()
    lax.fori_loop(1, 8, kv_start, 0)
    kv_pass(0).start()

    half_depth = out_proj.shape[0] // 2
    tops = [pl.ds(0, half_depth), pl.ds(half_depth, half_depth)]
    w_across = [begin(out_proj.at[top, :], weights.at[mine, top, :], across) for top in tops]
    w_pair = begin(out_proj, weights.at[mine], sibling)

    lax.fori_loop(1, 8, kv_forward, 0)
    lax.fori_loop(0, 8, kv_arrive, 0)
    loads[2].wait()

    scaling = head_width ** (-0.5)
    allowed = lax.broadcasted_iota(jnp.int32, (seq_rows, length), 1) <= (
        lax.broadcasted_iota(jnp.int32, (seq_rows, length), 0) + me * seq_rows
    )

    def att_copy(head, step):
        span = pl.ds(pl.multiple_of(head * head_width, 128), head_width)
        index = step * heads + head
        return remote(
            attended.at[0, :, span],
            attended.at[Z - step, :, span],
            att_send.at[index],
            att_recv.at[index],
            z_peer(step),
        )

    far = remote(
        attended.at[0], attended.at[2], att_send.at[0], att_recv.at[0], z_peer(2)
    )

    def one_head(head, carry):
        span = pl.ds(pl.multiple_of(head * head_width, 128), head_width)
        all_keys = pairs[:, :, 0:head_width].reshape(length, head_width)
        scores = contract_last(held_queries[:, span], all_keys) * scaling
        scores = jnp.where(allowed, scores, -1e30)
        highest = jnp.max(scores, axis=1, keepdims=True)
        probs = jnp.exp(scores - highest)
        totals = jnp.sum(probs, axis=1, keepdims=True)
        all_values = pairs[:, :, head_width : 2 * head_width].reshape(length, head_width)
        summed = dot(probs.astype(bf16), all_values)
        attended[0, :, span] = (summed / totals).astype(bf16)
        for step in (1, 3):
            att_copy(head, step).start()
        return carry

    lax.fori_loop(0, heads, one_head, 0)

    far.start()

    def halves(chunk):
        return pl.ds(pl.multiple_of(chunk * 2 * columns, 128), 2 * columns)

    chunks = (x_hi, 1 - x_hi)
    order = [(0, 0), (1, 0), (3, 0), (0, 1), (1, 1), (3, 1), (2, 0), (2, 1)]

    def part_copy(place, which, step):
        span = halves(chunks[which])
        index = (place * 2 + which) * exps + step
        return remote(
            part_send.at[lax.rem(exp + step, exps), place, :, span],
            part_recv.at[exp, place, :, span],
            part_send_sem.at[index],
            part_recv_sem.at[index],
            exp_peer(step),
        )

    def project(place, which):
        for piece in range(2):
            block = chunks[which] * 2 + piece
            at = pl.ds(pl.multiple_of(block * columns, 128), columns)
            value = dot(attended[place], weights[block]).astype(bf16)
            for exp_to in range(exps):
                part_send[exp_to, place, :, at] = value[exp_to * tokens : (exp_to + 1) * tokens]

        def part_start(step, carry):
            part_copy(place, which, step).start()
            return carry

        lax.fori_loop(1, exps, part_start, 0)

    def proj_copy(place, which):
        span = halves(chunks[which])
        index = place * 2 + which
        return remote(
            proj_send.at[place, :, span],
            proj.at[z, :, span],
            proj_send_sem.at[index],
            proj_recv_sem.at[index],
            z_peer(place),
        )

    def total_of(place, which):
        def part_arrive(step, carry):
            part_copy(place, which, step).wait_recv()
            return carry

        lax.fori_loop(1, exps, part_arrive, 0)
        span = halves(chunks[which])

        def add(step, total):
            return total + part_recv[lax.rem(exp + step, exps), place, :, span].astype(f32)

        total = lax.fori_loop(1, exps, add, part_send[exp, place, :, span].astype(f32))
        if place == 0:
            proj[z, :, span] = total.astype(bf16)
        else:
            proj_send[place, :, span] = total.astype(bf16)
            proj_copy(place, which).start()

    def rows_arrive(place):
        def att_arrive(head, carry):
            att_copy(head, Z - place).wait_recv()
            return carry

        lax.fori_loop(0, heads, att_arrive, 0)

    loads[3].wait()
    w_pair.wait_recv()
    project(0, 0)
    rows_arrive(1)
    project(1, 0)
    rows_arrive(3)
    project(3, 0)
    w_pass = []
    for index, top in enumerate(tops):
        w_across[index].wait_recv()
        at = weights.at[other, top, :]
        w_pass.append(begin(at, at, sibling))
    for copy in w_pass:
        copy.wait_recv()
    project(0, 1)
    project(1, 1)
    project(3, 1)
    far.wait_recv()
    project(2, 0)
    project(2, 1)
    for place, which in order:
        total_of(place, which)
    loads[4].wait()
    for place, which in order:
        if place > 0:
            proj_copy(place, which).wait_recv()
    for place in range(Z):
        span = slice(place * 4 * columns, (place + 1) * 4 * columns)
        out[:, span] = (held_residual[:, span].astype(f32) + proj[place].astype(f32)).astype(bf16)

    lax.fori_loop(1, 8, kv_sent, 0)
    kv_pass(0).wait_send()
    for copy in started:
        copy.wait_send()

    def att_sent(head, carry):
        for step in (1, 3):
            att_copy(head, step).wait_send()
        return carry

    lax.fori_loop(0, heads, att_sent, 0)
    far.wait_send()

    for place, which in order:

        def part_sent(step, carry, place=place, which=which):
            part_copy(place, which, step).wait_send()
            return carry

        lax.fori_loop(1, exps, part_sent, 0)
        if place > 0:
            proj_copy(place, which).wait_send()


def attention_layer(queries, key_heads, value_heads, out_proj, residual):
    bf16 = jnp.bfloat16
    tokens, width = residual.shape
    seq_rows, columns = queries.shape[0], out_proj.shape[1]
    exps = seq_rows // tokens
    head_width = key_heads.shape[1]
    heads = queries.shape[1] // head_width
    dma = pltpu.SemaphoreType.DMA
    vmem = pl.BlockSpec(memory_space=pltpu.VMEM)
    return pl.pallas_call(
        functools.partial(attention_kernel, exps),
        out_shape=jax.ShapeDtypeStruct((tokens, width), bf16),
        in_specs=[pl.BlockSpec(memory_space=pl.ANY)] * 5,
        out_specs=vmem,
        scratch_shapes=[
            pltpu.VMEM(queries.shape, bf16),
            pltpu.VMEM(residual.shape, bf16),
            pltpu.VMEM((16, seq_rows, 2 * head_width), bf16),
            pltpu.VMEM((4,) + out_proj.shape, bf16),
            pltpu.VMEM((Z, seq_rows, heads * head_width), bf16),
            pltpu.VMEM((exps, Z, tokens, 4 * columns), bf16),
            pltpu.VMEM((exps, Z, tokens, 4 * columns), bf16),
            pltpu.VMEM((Z, tokens, 4 * columns), bf16),
            pltpu.VMEM((Z, tokens, 4 * columns), bf16),
            dma((8,)),
            dma((8,)),
            dma((8,)),
            dma((8,)),
            dma((5,)),
            dma((5,)),
            dma((4 * heads,)),
            dma((4 * heads,)),
            dma((8 * exps,)),
            dma((8 * exps,)),
            dma((2 * Z,)),
            dma((2 * Z,)),
            dma((5,)),
        ],
        compiler_params=pltpu.CompilerParams(
            collective_id=2, has_side_effects=True, vmem_limit_bytes=62 * 2**20
        ),
    )(queries, key_heads, value_heads, out_proj, residual)


def on_device(
    residual,
    queries,
    key_heads,
    value_heads,
    out_proj,
    norm_gain,
    gate_weight,
    up_weight,
    down_weight,
    adapter_in,
    adapter_out,
    route_ids,
    route_gates,
    adapter_mix,
):
    hidden_state = attention_layer(queries, key_heads, value_heads, out_proj, residual)
    return expert_layer(
        hidden_state,
        norm_gain,
        route_ids,
        route_gates,
        adapter_mix,
        gate_weight[0],
        up_weight[0],
        down_weight[0],
        adapter_in[0],
        adapter_out[0],
        lax.axis_size("exp"),
    )


def solution(mesh):
    in_specs = (
        P(("seq", "exp"), None),
        P("seq", "exp"),
        P("seq", "exp"),
        P("seq", "exp"),
        P("exp", "seq"),
        P(),
        P("exp", "seq", None),
        P("exp", "seq", None),
        P("exp", "seq", None),
        P("exp", "seq", None),
        P("exp", "seq", None),
        P(("seq", "exp"), None),
        P(("seq", "exp"), None),
        P(("seq", "exp"), None),
    )
    out_specs = P(("seq", "exp"), None)
    return jax.shard_map(
        on_device, mesh=mesh, in_specs=in_specs, out_specs=out_specs, check_vma=False
    )
```

```python
import functools

import jax
import jax.numpy as jnp
from jax import lax
from jax.experimental import pallas as pl
from jax.experimental.pallas import tpu as pltpu
from jax.sharding import PartitionSpec as P

RANK = 16


MESH = pl.DeviceIdType.MESH
CAP = 5
Z = 4
PIECES = 3
SLOT_ROWS = 16


def dot(left, right):
    return jnp.dot(left, right, preferred_element_type=jnp.float32)


def contract_last(left, right):
    return lax.dot_general(
        left, right, (((1,), (1,)), ((), ())), preferred_element_type=jnp.float32
    )


def tile_of(size, most):
    while size % most:
        most -= 128
    return most


def place_on_mesh():
    me = lax.axis_index("seq")
    core = lax.rem(me, 2)
    x_hi = lax.rem(me // 2, 2)
    z = me // 4
    return me, z, x_hi, core


def seq_of(z, x_hi, core):
    return lax.rem(z + Z, Z) * 4 + x_hi * 2 + core


def expert_kernel(
    exps,
    hidden,
    gain,
    ids,
    route_gates,
    mix,
    gate_hbm,
    up_hbm,
    down_hbm,
    in_hbm,
    out_hbm,
    out,
    placed_wide,
    disp,
    arrived,
    wide_slots,
    rows,
    w_first,
    w_second,
    units,
    pair_send,
    pair_recv,
    own,
    z_send,
    half_low,
    half_high,
    full_low,
    full_high,
    x_send,
    x_recv,
    wide_send,
    wide_recv,
    back_wide,
    back,
    returned,
    returned_wide,
    returned_rows,
    weight_sems,
    send_sems,
    recv_sems,
    disp_send,
    disp_recv,
    back_send,
    back_recv,
    local_sems,
):
    bf16, f32 = jnp.bfloat16, jnp.float32
    tokens, width = hidden.shape
    half = width // 2
    lanes = half // 128
    run = lanes // PIECES
    piece = run * 128
    hidden_units = gate_hbm.shape[0]
    adapters = in_hbm.shape[0]
    block = 2 * exps * CAP
    many = 4 * block
    peers = 2 * exps
    slots = exps * CAP
    mix_width = mix.shape[1]

    me, z, x_hi, core = place_on_mesh()
    exp = lax.axis_index("exp")
    sibling = (seq_of(z, x_hi, 1 - core), exp)
    above = (seq_of(z + 1, x_hi, core), exp)
    below = (seq_of(z - 1, x_hi, core), exp)
    across = (seq_of(z, 1 - x_hi, core), exp)
    mine = core * exps + exp

    def peer(step):
        at = lax.rem(mine + step, peers)
        return at, (seq_of(z, x_hi, at // exps), lax.rem(at, exps))

    barrier = pltpu.get_barrier_semaphore()

    def greet(step, carry):
        pl.semaphore_signal(barrier, inc=1, device_id=peer(step)[1], device_id_type=MESH)
        return carry

    lax.fori_loop(1, peers, greet, 0)
    for other in (above, below, across):
        pl.semaphore_signal(barrier, inc=1, device_id=other, device_id_type=MESH)

    loads = []
    for side in range(2):
        columns = pl.ds(side * half, half)
        for source, place, start in (
            (gate_hbm, w_first, 0),
            (up_hbm, w_first, hidden_units),
            (in_hbm, w_first, 2 * hidden_units),
            (down_hbm, w_second, 0),
            (out_hbm, w_second, hidden_units),
        ):
            load = pltpu.make_async_copy(
                source.at[:, columns],
                place.at[side, pl.ds(start, source.shape[0]), :],
                weight_sems.at[len(loads)],
            )
            load.start()
            loads.append(load)

    first_row, second_row = ids[0:1, :], ids[1:2, :]
    down_at = lax.broadcasted_iota(jnp.int32, (tokens, tokens), 0)
    along_at = lax.broadcasted_iota(jnp.int32, (tokens, tokens), 1)

    def upright(row):
        return jnp.sum(jnp.where(down_at == along_at, row, 0), axis=1, keepdims=True)

    first, second = upright(first_row), upright(second_row)

    def count(hits, axis):
        return jnp.sum(jnp.where(hits, 1, 0), axis=axis, keepdims=True)

    first_slot_row = first_row * CAP + count((first == first_row) & (down_at < along_at), 0)
    second_slot_row = (
        second_row * CAP
        + count(first == second_row, 0)
        + count((second == second_row) & (down_at < along_at), 0)
    )
    first_slot = first * CAP + count((first == first_row) & (along_at < down_at), 1)
    second_slot = (
        second * CAP
        + count(second == first_row, 1)
        + count((second == second_row) & (along_at < down_at), 1)
    )
    slot_at = lax.broadcasted_iota(jnp.int32, (slots, tokens), 0)
    placing = jnp.where(
        (slot_at == first_slot_row) | (slot_at == second_slot_row), 1.0, 0.0
    ).astype(bf16)
    slot_along = lax.broadcasted_iota(jnp.int32, (tokens, slots), 1)
    slot_gates = jnp.where(slot_along == first_slot, upright(route_gates[0:1, :]), 0.0) + jnp.where(
        slot_along == second_slot, upright(route_gates[1:2, :]), 0.0
    )
    gate_high = slot_gates.astype(bf16)
    rest = slot_gates - gate_high.astype(f32)
    gate_mid = rest.astype(bf16)
    gate_low = (rest - gate_mid.astype(f32)).astype(bf16)

    wide = hidden[...].astype(f32)
    scale = lax.rsqrt(jnp.mean(wide * wide, axis=1, keepdims=True) + 1e-05)

    def place_columns(side, lane):
        columns = slice(side * half + lane * 128, side * half + (lane + 1) * 128)
        normed = (hidden[:, columns].astype(f32) * scale * gain[:, columns]).astype(bf16)
        return dot(placing, normed)

    placed_wide[...] = jnp.zeros_like(placed_wide)
    mix_rows = dot(placing, mix[...].astype(f32).astype(bf16))
    for side in range(2):
        for lane in range(lanes):
            part, at = (0, lane) if lane < run else (1, lane - run)
            start = (side * 2 + part) * slots * SLOT_ROWS + at
            placed_wide[pl.ds(start, slots, stride=SLOT_ROWS), :] = place_columns(side, lane)
        start = side * 2 * slots * SLOT_ROWS + run
        placed_wide[pl.ds(start, slots, stride=SLOT_ROWS), 0:mix_width] = mix_rows
    disp[...] = placed_wide[...].reshape(disp.shape).astype(bf16)

    pl.semaphore_wait(barrier, peers - 1 + 3)

    def remote(source, target, send, recv, device):
        return pltpu.make_async_remote_copy(
            src_ref=source,
            dst_ref=target,
            send_sem=send,
            recv_sem=recv,
            device_id=device,
            device_id_type=MESH,
        )

    started = []

    def begin(source, target, device):
        index = len(started)
        copy = remote(source, target, send_sems.at[index], recv_sems.at[index], device)
        copy.start()
        started.append(copy)
        return copy

    def dispatch(part, step):
        at, device = peer(step)
        return remote(
            disp.at[at // exps, part, lax.rem(at, exps)],
            arrived.at[part, mine],
            disp_send.at[part, step],
            disp_recv.at[part, step],
            device,
        )

    keeps = []
    for part in range(2):

        def dispatch_start(step, carry, part=part):
            dispatch(part, step).start()
            return carry

        lax.fori_loop(1, peers, dispatch_start, 0)
        keep = pltpu.make_async_copy(
            disp.at[core, part, exp], arrived.at[part, mine], local_sems.at[part]
        )
        keep.start()
        keeps.append(keep)

    edges = [0] + [128 + (index + 1) * piece for index in range(PIECES)]
    middles = [
        edges[index] + (edges[index + 1] - edges[index]) // 256 * 128 for index in range(PIECES)
    ]

    def land(part):
        def dispatch_wait(step, carry):
            dispatch(part, step).wait_recv()
            return carry

        lax.fori_loop(1, peers, dispatch_wait, 0)
        keeps[part].wait()
        wide_slots[part] = arrived[part].astype(f32).reshape(block * SLOT_ROWS, 128)
        chosen = [(run, 0)] + [(lane, lane + 1) for lane in range(run)]
        if part == 1:
            chosen = [(lane, run + 1 + lane) for lane in range(lanes - run)]
        for source, target in chosen:
            rows[core, 0:block, target * 128 : (target + 1) * 128] = wide_slots[
                part, pl.ds(source, block, stride=SLOT_ROWS), :
            ].astype(bf16)

    def cell(place, start, stop):
        return rows.at[core, pl.ds(place * block, block), pl.ds(start, stop - start)]

    def move(source, target, index, device, which=None):
        start, stop = edges[index], edges[index + 1]
        if which == 0:
            stop = middles[index]
        if which == 1:
            start = middles[index]
        return begin(cell(source, start, stop), cell(target, start, stop), device)

    handed = {}

    def hand_over(place, index):
        handed[place, index] = move(place, place, index, sibling)

    low, high, opposite, crossed = {}, {}, {}, {}

    def ring_own(index):
        low[0, index] = move(0, 1, index, above)
        high[0, index] = move(0, 2, index, below)

    def cross_own(index):
        crossed[0, index] = move(0, 4, index, across)
        hand_over(0, index)

    def relay(base, index):
        low[base, index].wait_recv()
        opposite[base, index, 0] = move(base + 1, base + 3, index, above, 0)
        if index == 0:
            crossed[1, 0] = move(1, 5, 0, across)
        hand_over(base + 1, index)
        high[base, index].wait_recv()
        opposite[base, index, 1] = move(base + 2, base + 3, index, below, 1)
        if index == 0:
            crossed[2, 0] = move(2, 6, 0, across)
        hand_over(base + 2, index)

    def close(base, index):
        opposite[base, index, 0].wait_recv()
        opposite[base, index, 1].wait_recv()
        if index == 0:
            crossed[3, 0] = move(3, 7, 0, across)
        hand_over(base + 3, index)

    def spread_crossed(index):
        crossed[0, index].wait_recv()
        low[4, index] = move(4, 5, index, above)
        high[4, index] = move(4, 6, index, below)
        hand_over(4, index)

    def take_crossed(place):
        crossed[place, 0].wait_recv()
        hand_over(place + 4, 0)

    land(0)
    ring_own(0)
    cross_own(0)
    land(1)
    for index in range(1, PIECES):
        cross_own(index)
    ring_own(1)
    relay(0, 0)
    spread_crossed(1)
    spread_crossed(2)
    ring_own(2)
    close(0, 0)
    relay(4, 1)
    relay(4, 2)
    for place in range(4):
        take_crossed(place)
    for index in range(1, PIECES):
        close(4, index)

    for load in loads:
        load.wait()
    unit_tile = tile_of(hidden_units, 256)
    adapter_at = lax.broadcasted_iota(jnp.int32, (mix_width, adapters), 1) // RANK
    spread = (
        lax.broadcasted_iota(jnp.int32, (mix_width, adapters), 0)
        == adapter_at + me * (adapters // RANK)
    ).astype(bf16)

    def first_layer(group, between):
        at = pl.ds(group * many, many)
        data = pl.ds(128, half)

        def project(start, size):
            return contract_last(
                rows[0, at, data], w_first[0, pl.ds(start, size), :]
            ) + contract_last(rows[1, at, data], w_first[1, pl.ds(start, size), :])

        scales = dot(rows[0, at, 0:mix_width], spread) / 8.0
        units[:, hidden_units : hidden_units + adapters] = (
            project(2 * hidden_units, adapters) * scales
        ).astype(bf16)
        for start in range(0, hidden_units, unit_tile):
            gate = project(start, unit_tile)
            between[0]()
            upward = project(hidden_units + start, unit_tile)
            units[:, start : start + unit_tile] = (jax.nn.silu(gate) * upward).astype(bf16)
            between[1]()
            between = between[2:]

    out_tile = tile_of(piece, 1024)

    def second_layer(group, side, index, target):
        def tile(step, carry):
            start = pl.multiple_of(index * piece + step * out_tile, 128)
            value = dot(units[...], w_second[side, :, pl.ds(start, out_tile)])
            target[group, :, pl.ds(start, out_tile)] = value.astype(target.dtype)
            return carry

        lax.fori_loop(0, piece // out_tile, tile, 0)

    def columns_of(index, which=None):
        start, stop = index * piece, (index + 1) * piece
        middle = start + piece // 256 * 128
        if which == 0:
            stop = middle
        if which == 1:
            start = middle
        return pl.ds(start, stop - start)

    swaps = {}

    def to_sibling(group, index):
        second_layer(group, 1 - core, index, pair_send)
        at = columns_of(index)
        swaps[group, index] = begin(
            pair_send.at[group, :, at], pair_recv.at[group, :, at], sibling
        )

    def pair_sum(group, place, index, which=None):
        columns = columns_of(index, which)
        inner = columns_of(0, which)
        at = pl.ds(place * block, block)
        total = own[group, at, columns] + pair_recv[group, at, columns].astype(f32)
        if group == 0 and index == 0:
            total = total + wide_recv[at, inner].astype(f32)
        return total

    flows = {}

    def z_flow(group, index, place, which, target, device):
        at = columns_of(index, which)
        return begin(z_send.at[group, place - 1, :, at], target.at[group, :, at], device)

    def reduce_own(group, index):
        second_layer(group, core, index, own)
        swaps[group, index].wait_recv()
        both, left, right = (columns_of(index, which) for which in (None, 0, 1))
        z_send[group, 2, :, both] = pair_sum(group, 3, index).astype(bf16)
        flows["half_low", group, index] = z_flow(group, index, 3, 0, half_low, above)
        flows["half_high", group, index] = z_flow(group, index, 3, 1, half_high, below)
        z_send[group, 1, :, right] = pair_sum(group, 2, index, 1).astype(bf16)
        flows["low_1", group, index] = z_flow(group, index, 2, 1, full_low, above)
        z_send[group, 0, :, left] = pair_sum(group, 1, index, 0).astype(bf16)
        flows["high_0", group, index] = z_flow(group, index, 1, 0, full_high, below)
        own[group, 2 * block : 3 * block, left] = pair_sum(group, 2, index, 0)
        own[group, block : 2 * block, right] = pair_sum(group, 1, index, 1)
        own[group, 0:block, both] = pair_sum(group, 0, index)

    def pass_on(group, index):
        left, right = columns_of(index, 0), columns_of(index, 1)
        flows["half_low", group, index].wait_recv()
        z_send[group, 1, :, left] = (
            own[group, 2 * block : 3 * block, left] + half_low[group, :, left].astype(f32)
        ).astype(bf16)
        flows["low_0", group, index] = z_flow(group, index, 2, 0, full_low, above)
        flows["half_high", group, index].wait_recv()
        z_send[group, 0, :, right] = (
            own[group, block : 2 * block, right] + half_high[group, :, right].astype(f32)
        ).astype(bf16)
        flows["high_1", group, index] = z_flow(group, index, 1, 1, full_high, below)

    def settled(group, index):
        for name in ("low_0", "low_1", "high_0", "high_1"):
            flows[name, group, index].wait_recv()
        both = columns_of(index)
        return (
            own[group, 0:block, both]
            + full_low[group, :, both].astype(f32)
            + full_high[group, :, both].astype(f32)
        )

    def all_here(group):
        for place in range(4):
            for index in range(PIECES):
                handed[group * 4 + place, index].wait_recv()

    def nothing():
        return None

    def cross_wide():
        second_layer(1, core, 0, own)
        swaps[1, 0].wait_recv()
        for place in range(4):
            wide_send[place * block : (place + 1) * block, :] = pair_sum(
                1, place, 0
            ).astype(bf16)
        flows["wide"] = begin(wide_send, wide_recv, across)

    crossing = {}

    def cross_settled(index):
        at = columns_of(index)
        x_send[:, at] = settled(1, index).astype(bf16)
        crossing[index] = begin(x_send.at[:, at], x_recv.at[:, at], across)

    all_here(1)
    first_layer(
        1,
        [lambda: relay(0, 1), nothing, lambda: relay(0, 2), nothing],
    )
    to_sibling(1, 0)
    to_sibling(1, 1)
    cross_wide()
    to_sibling(1, 2)
    close(0, 1)
    reduce_own(1, 1)
    close(0, 2)
    reduce_own(1, 2)
    all_here(0)
    first_layer(
        0,
        [lambda: pass_on(1, 1), nothing, lambda: pass_on(1, 2), nothing],
    )
    to_sibling(0, 1)
    to_sibling(0, 2)
    reduce_own(0, 1)
    to_sibling(0, 0)
    reduce_own(0, 2)
    cross_settled(1)
    flows["wide"].wait_recv()
    reduce_own(0, 0)
    cross_settled(2)
    for index in (1, 2, 0):
        pass_on(0, index)

    def give_back(index, step):
        at, device = peer(step)
        return remote(
            back.at[index, at],
            returned.at[index, core, exp],
            back_send.at[index, step],
            back_recv.at[index, step],
            device,
        )

    keeps_back = {}
    for index in (1, 2, 0):
        own[0, 0:block, columns_of(index)] = settled(0, index)
        if index > 0:
            crossing[index].wait_recv()
        for lane in range(run):
            columns = slice(index * piece + lane * 128, index * piece + (lane + 1) * 128)
            value = own[0, 0:block, columns]
            if index > 0:
                value = value + x_recv[:, columns].astype(f32)
            back_wide[index, pl.ds(lane, block, stride=run), :] = value
        back[index] = back_wide[index].reshape(back.shape[1:]).astype(bf16)

        def give_start(step, carry, index=index):
            give_back(index, step).start()
            return carry

        lax.fori_loop(1, peers, give_start, 0)
        keep = pltpu.make_async_copy(
            back.at[index, mine], returned.at[index, core, exp], local_sems.at[2 + index]
        )
        keep.start()
        keeps_back[index] = keep

    for copy in started:
        copy.wait_send()
    for part in range(2):

        def dispatch_sent(step, carry, part=part):
            dispatch(part, step).wait_send()
            return carry

        lax.fori_loop(1, peers, dispatch_sent, 0)
    stacked = jnp.concatenate(
        [gate_high.astype(f32), gate_mid.astype(f32), gate_low.astype(f32)], axis=0
    ).astype(bf16)
    for index in (1, 2, 0):

        def give_wait(step, carry, index=index):
            give_back(index, step).wait()
            return carry

        lax.fori_loop(1, peers, give_wait, 0)
        keeps_back[index].wait()
        returned_wide[...] = returned[index].astype(f32).reshape(2 * slots * run, 128)
        for side in range(2):
            for lane in range(run):
                returned_rows[side, :, lane * 128 : (lane + 1) * 128] = returned_wide[
                    pl.ds(side * slots * run + lane, slots, stride=run), :
                ].astype(bf16)
            routed = dot(stacked, returned_rows[side])
            routed = routed[0:tokens] + (
                routed[tokens : 2 * tokens] + routed[2 * tokens : 3 * tokens]
            )
            columns = slice(side * half + index * piece, side * half + (index + 1) * piece)
            out[:, columns] = (hidden[:, columns].astype(f32) + routed).astype(bf16)


def expert_layer(
    hidden, gain, ids, route_gates, mix, gate, up, down, adapter_in, adapter_out, exps
):
    bf16, f32 = jnp.bfloat16, jnp.float32
    tokens, width = hidden.shape
    half = width // 2
    lanes = half // 128
    run = lanes // PIECES
    block = 2 * exps * CAP
    slots = exps * CAP
    hidden_units, adapters = gate.shape[0], adapter_in.shape[0]
    inner = hidden_units + adapters
    dma = pltpu.SemaphoreType.DMA
    vmem = pl.BlockSpec(memory_space=pltpu.VMEM)
    anywhere = pl.BlockSpec(memory_space=pl.ANY)
    return pl.pallas_call(
        functools.partial(expert_kernel, exps),
        out_shape=jax.ShapeDtypeStruct((tokens, width), bf16),
        in_specs=[vmem] * 5 + [anywhere] * 5,
        out_specs=vmem,
        scratch_shapes=[
            pltpu.VMEM((2 * 2 * slots * SLOT_ROWS, 128), f32),
            pltpu.VMEM((2, 2, exps, CAP, SLOT_ROWS, 128), bf16),
            pltpu.VMEM((2, 2 * exps, CAP, SLOT_ROWS, 128), bf16),
            pltpu.VMEM((2, block * SLOT_ROWS, 128), f32),
            pltpu.VMEM((2, 8 * block, half + 128), bf16),
            pltpu.VMEM((2, hidden_units + inner, half), bf16),
            pltpu.VMEM((2, inner, half), bf16),
            pltpu.VMEM((4 * block, inner), bf16),
            pltpu.VMEM((2, 4 * block, half), bf16),
            pltpu.VMEM((2, 4 * block, half), bf16),
            pltpu.VMEM((2, 4 * block, half), f32),
            pltpu.VMEM((2, 3, block, half), bf16),
            pltpu.VMEM((2, block, half), bf16),
            pltpu.VMEM((2, block, half), bf16),
            pltpu.VMEM((2, block, half), bf16),
            pltpu.VMEM((2, block, half), bf16),
            pltpu.VMEM((block, half), bf16),
            pltpu.VMEM((block, half), bf16),
            pltpu.VMEM((4 * block, run * 128), bf16),
            pltpu.VMEM((4 * block, run * 128), bf16),
            pltpu.VMEM((PIECES, block * run, 128), f32),
            pltpu.VMEM((PIECES, 2 * exps, CAP, run, 128), bf16),
            pltpu.VMEM((PIECES, 2, exps, CAP, run, 128), bf16),
            pltpu.VMEM((2 * slots * run, 128), f32),
            pltpu.VMEM((2, slots, run * 128), bf16),
            dma((10,)),
            dma((108,)),
            dma((108,)),
            dma((2, 2 * exps)),
            dma((2, 2 * exps)),
            dma((PIECES, 2 * exps)),
            dma((PIECES, 2 * exps)),
            dma((2 + PIECES,)),
        ],
        compiler_params=pltpu.CompilerParams(
            collective_id=1, has_side_effects=True, vmem_limit_bytes=62 * 2**20
        ),
    )(
        hidden,
        gain.reshape(1, width),
        ids.T,
        route_gates.T,
        mix,
        gate,
        up,
        down,
        adapter_in,
        adapter_out,
    )


def attention_kernel(
    exps,
    queries,
    key_heads,
    value_heads,
    out_proj,
    residual,
    out,
    held_queries,
    held_residual,
    pairs,
    weights,
    attended,
    part_send,
    part_recv,
    proj_send,
    proj,
    kv_send,
    kv_recv,
    pass_send,
    pass_recv,
    send_sems,
    recv_sems,
    att_send,
    att_recv,
    part_send_sem,
    part_recv_sem,
    proj_send_sem,
    proj_recv_sem,
    local_sems,
):
    bf16, f32 = jnp.bfloat16, jnp.float32
    seq_rows = queries.shape[0]
    head_width = key_heads.shape[1]
    heads = queries.shape[1] // head_width
    tokens = seq_rows // exps
    columns = out_proj.shape[1]
    length = 16 * seq_rows

    me, z, x_hi, core = place_on_mesh()
    exp = lax.axis_index("exp")
    sibling = (seq_of(z, x_hi, 1 - core), exp)
    across = (seq_of(z, 1 - x_hi, core), exp)
    chip = z * 2 + x_hi
    mine = x_hi * 2 + core
    other = (1 - x_hi) * 2 + core

    def z_peer(step):
        return seq_of(z + step, x_hi, core), exp

    def exp_peer(step):
        return me, lax.rem(exp + step, exps)

    barrier = pltpu.get_barrier_semaphore()

    def greet_exp(step, carry):
        pl.semaphore_signal(barrier, inc=1, device_id=exp_peer(step), device_id_type=MESH)
        return carry

    def chip_peer(step):
        return lax.rem(chip + step, 8) * 2 + core, exp

    def greet_chip(step, carry):
        pl.semaphore_signal(barrier, inc=1, device_id=chip_peer(step), device_id_type=MESH)
        return carry

    pairs[...] = jnp.zeros_like(pairs)
    pl.semaphore_signal(barrier, inc=1, device_id=sibling, device_id_type=MESH)
    lax.fori_loop(1, 8, greet_chip, 0)
    lax.fori_loop(1, exps, greet_exp, 0)
    loads = []
    for source, target in (
        (key_heads, pairs.at[me, :, pl.ds(0, head_width)]),
        (value_heads, pairs.at[me, :, pl.ds(head_width, head_width)]),
        (queries, held_queries),
        (out_proj, weights.at[mine]),
        (residual, held_residual),
    ):
        load = pltpu.make_async_copy(source, target, local_sems.at[len(loads)])
        load.start()
        loads.append(load)
    pl.semaphore_wait(barrier, 1 + 7 + exps - 1)

    def remote(source, target, send, recv, device):
        return pltpu.make_async_remote_copy(
            src_ref=source,
            dst_ref=target,
            send_sem=send,
            recv_sem=recv,
            device_id=device,
            device_id_type=MESH,
        )

    started = []

    def begin(source, target, device):
        index = len(started)
        copy = remote(source, target, send_sems.at[index], recv_sems.at[index], device)
        copy.start()
        started.append(copy)
        return copy

    def kv_copy(step):
        return remote(
            pairs.at[me], pairs.at[me], kv_send.at[step], kv_recv.at[step], chip_peer(step)
        )

    def kv_pass(step):
        at = lax.rem(chip - step + 8, 8) * 2 + core
        return remote(pairs.at[at], pairs.at[at], pass_send.at[step], pass_recv.at[step], sibling)

    def kv_start(step, carry):
        @pl.when(chip + step < 8)
        def _():
            kv_copy(step).start()

        return carry

    def kv_forward(step, carry):
        @pl.when(chip - step >= 0)
        def _():
            kv_copy(step).wait_recv()
            kv_pass(step).start()

        return carry

    def kv_arrive(step, carry):
        @pl.when(chip - step >= 0)
        def _():
            kv_pass(step).wait_recv()

        return carry

    def kv_sent(step, carry):
        @pl.when(chip + step < 8)
        def _():
            kv_copy(step).wait_send()

        @pl.when(chip - step >= 0)
        def _():
            kv_pass(step).wait_send()

        return carry

    loads[0].wait()
    loads[1].wait()
    lax.fori_loop(1, 8, kv_start, 0)
    kv_pass(0).start()

    half_depth = out_proj.shape[0] // 2
    tops = [pl.ds(0, half_depth), pl.ds(half_depth, half_depth)]
    w_across = [begin(out_proj.at[top, :], weights.at[mine, top, :], across) for top in tops]
    w_pair = begin(out_proj, weights.at[mine], sibling)

    lax.fori_loop(1, 8, kv_forward, 0)
    lax.fori_loop(0, 8, kv_arrive, 0)
    loads[2].wait()

    scaling = head_width ** (-0.5)
    allowed = lax.broadcasted_iota(jnp.int32, (seq_rows, length), 1) <= (
        lax.broadcasted_iota(jnp.int32, (seq_rows, length), 0) + me * seq_rows
    )

    def att_copy(head, step):
        span = pl.ds(pl.multiple_of(head * head_width, 128), head_width)
        index = step * heads + head
        return remote(
            attended.at[0, :, span],
            attended.at[Z - step, :, span],
            att_send.at[index],
            att_recv.at[index],
            z_peer(step),
        )

    far = remote(
        attended.at[0], attended.at[2], att_send.at[0], att_recv.at[0], z_peer(2)
    )

    def one_head(head, carry):
        span = pl.ds(pl.multiple_of(head * head_width, 128), head_width)
        all_keys = pairs[:, :, 0:head_width].reshape(length, head_width)
        scores = contract_last(held_queries[:, span], all_keys) * scaling
        scores = jnp.where(allowed, scores, -1e30)
        highest = jnp.max(scores, axis=1, keepdims=True)
        probs = jnp.exp(scores - highest)
        totals = jnp.sum(probs, axis=1, keepdims=True)
        all_values = pairs[:, :, head_width : 2 * head_width].reshape(length, head_width)
        summed = dot(probs.astype(bf16), all_values)
        attended[0, :, span] = (summed / totals).astype(bf16)
        for step in (1, 3):
            att_copy(head, step).start()
        return carry

    lax.fori_loop(0, heads, one_head, 0)

    far.start()

    def halves(chunk):
        return pl.ds(pl.multiple_of(chunk * 2 * columns, 128), 2 * columns)

    chunks = (x_hi, 1 - x_hi)
    order = [(0, 0), (1, 0), (3, 0), (0, 1), (1, 1), (3, 1), (2, 0), (2, 1)]

    def part_copy(place, which, step):
        span = halves(chunks[which])
        index = (place * 2 + which) * exps + step
        return remote(
            part_send.at[lax.rem(exp + step, exps), place, :, span],
            part_recv.at[exp, place, :, span],
            part_send_sem.at[index],
            part_recv_sem.at[index],
            exp_peer(step),
        )

    def project(place, which):
        for piece in range(2):
            block = chunks[which] * 2 + piece
            at = pl.ds(pl.multiple_of(block * columns, 128), columns)
            value = dot(attended[place], weights[block]).astype(bf16)
            for exp_to in range(exps):
                part_send[exp_to, place, :, at] = value[exp_to * tokens : (exp_to + 1) * tokens]

        def part_start(step, carry):
            part_copy(place, which, step).start()
            return carry

        lax.fori_loop(1, exps, part_start, 0)

    def proj_copy(place, which):
        span = halves(chunks[which])
        index = place * 2 + which
        return remote(
            proj_send.at[place, :, span],
            proj.at[z, :, span],
            proj_send_sem.at[index],
            proj_recv_sem.at[index],
            z_peer(place),
        )

    def total_of(place, which):
        def part_arrive(step, carry):
            part_copy(place, which, step).wait_recv()
            return carry

        lax.fori_loop(1, exps, part_arrive, 0)
        span = halves(chunks[which])

        def add(step, total):
            return total + part_recv[lax.rem(exp + step, exps), place, :, span].astype(f32)

        total = lax.fori_loop(1, exps, add, part_send[exp, place, :, span].astype(f32))
        if place == 0:
            proj[z, :, span] = total.astype(bf16)
        else:
            proj_send[place, :, span] = total.astype(bf16)
            proj_copy(place, which).start()

    def rows_arrive(place):
        def att_arrive(head, carry):
            att_copy(head, Z - place).wait_recv()
            return carry

        lax.fori_loop(0, heads, att_arrive, 0)

    loads[3].wait()
    w_pair.wait_recv()
    project(0, 0)
    rows_arrive(1)
    project(1, 0)
    rows_arrive(3)
    project(3, 0)
    w_pass = []
    for index, top in enumerate(tops):
        w_across[index].wait_recv()
        at = weights.at[other, top, :]
        w_pass.append(begin(at, at, sibling))
    for copy in w_pass:
        copy.wait_recv()
    project(0, 1)
    project(1, 1)
    project(3, 1)
    far.wait_recv()
    project(2, 0)
    project(2, 1)
    for place, which in order:
        total_of(place, which)
    loads[4].wait()
    for place, which in order:
        if place > 0:
            proj_copy(place, which).wait_recv()
    for place in range(Z):
        span = slice(place * 4 * columns, (place + 1) * 4 * columns)
        out[:, span] = (held_residual[:, span].astype(f32) + proj[place].astype(f32)).astype(bf16)

    lax.fori_loop(1, 8, kv_sent, 0)
    kv_pass(0).wait_send()
    for copy in started:
        copy.wait_send()

    def att_sent(head, carry):
        for step in (1, 3):
            att_copy(head, step).wait_send()
        return carry

    lax.fori_loop(0, heads, att_sent, 0)
    far.wait_send()

    for place, which in order:

        def part_sent(step, carry, place=place, which=which):
            part_copy(place, which, step).wait_send()
            return carry

        lax.fori_loop(1, exps, part_sent, 0)
        if place > 0:
            proj_copy(place, which).wait_send()


def attention_layer(queries, key_heads, value_heads, out_proj, residual):
    bf16 = jnp.bfloat16
    tokens, width = residual.shape
    seq_rows, columns = queries.shape[0], out_proj.shape[1]
    exps = seq_rows // tokens
    head_width = key_heads.shape[1]
    heads = queries.shape[1] // head_width
    dma = pltpu.SemaphoreType.DMA
    vmem = pl.BlockSpec(memory_space=pltpu.VMEM)
    return pl.pallas_call(
        functools.partial(attention_kernel, exps),
        out_shape=jax.ShapeDtypeStruct((tokens, width), bf16),
        in_specs=[pl.BlockSpec(memory_space=pl.ANY)] * 5,
        out_specs=vmem,
        scratch_shapes=[
            pltpu.VMEM(queries.shape, bf16),
            pltpu.VMEM(residual.shape, bf16),
            pltpu.VMEM((16, seq_rows, 2 * head_width), bf16),
            pltpu.VMEM((4,) + out_proj.shape, bf16),
            pltpu.VMEM((Z, seq_rows, heads * head_width), bf16),
            pltpu.VMEM((exps, Z, tokens, 4 * columns), bf16),
            pltpu.VMEM((exps, Z, tokens, 4 * columns), bf16),
            pltpu.VMEM((Z, tokens, 4 * columns), bf16),
            pltpu.VMEM((Z, tokens, 4 * columns), bf16),
            dma((8,)),
            dma((8,)),
            dma((8,)),
            dma((8,)),
            dma((5,)),
            dma((5,)),
            dma((4 * heads,)),
            dma((4 * heads,)),
            dma((8 * exps,)),
            dma((8 * exps,)),
            dma((2 * Z,)),
            dma((2 * Z,)),
            dma((5,)),
        ],
        compiler_params=pltpu.CompilerParams(
            collective_id=2, has_side_effects=True, vmem_limit_bytes=62 * 2**20
        ),
    )(queries, key_heads, value_heads, out_proj, residual)


def on_device(
    residual,
    queries,
    key_heads,
    value_heads,
    out_proj,
    norm_gain,
    gate_weight,
    up_weight,
    down_weight,
    adapter_in,
    adapter_out,
    route_ids,
    route_gates,
    adapter_mix,
):
    hidden_state = attention_layer(queries, key_heads, value_heads, out_proj, residual)
    return expert_layer(
        hidden_state,
        norm_gain,
        route_ids,
        route_gates,
        adapter_mix,
        gate_weight[0],
        up_weight[0],
        down_weight[0],
        adapter_in[0],
        adapter_out[0],
        lax.axis_size("exp"),
    )


def solution(mesh):
    in_specs = (
        P(("seq", "exp"), None),
        P("seq", "exp"),
        P("seq", "exp"),
        P("seq", "exp"),
        P("exp", "seq"),
        P(),
        P("exp", "seq", None),
        P("exp", "seq", None),
        P("exp", "seq", None),
        P("exp", "seq", None),
        P("exp", "seq", None),
        P(("seq", "exp"), None),
        P(("seq", "exp"), None),
        P(("seq", "exp"), None),
    )
    out_specs = P(("seq", "exp"), None)
    return jax.shard_map(
        on_device, mesh=mesh, in_specs=in_specs, out_specs=out_specs, check_vma=False
    )
```
